256 devices in a mesh: ep: 32 (over x, y, core), etp: 8 (over z).
Axes of the slice: x: 4, y: 4, z: 8, core: 2. Of those that a mesh axis runs over, the one named last changes fastest.
Arguments:
- tokens: bfloat16 [4096, 3584], P('ep'), may hold values from -6 to 6
- out_grad: bfloat16 [4096, 3584], P('ep'), may hold values from -6 to 6
- expert_ids: int32 [4096, 2], P('ep'), may hold values from 0 to 31, as said below
- route_probs: bfloat16 [4096, 2], P('ep'), may hold values from 0.099609375 to 1
- w_gate: bfloat16 [32, 3584, 3200], P('ep', None, 'etp'), may hold values from -0.09375 to 0.09375
- w_up: bfloat16 [32, 3584, 3200], P('ep', None, 'etp'), may hold values from -0.09375 to 0.09375
- w_down: bfloat16 [32, 3200, 3584], P('ep', 'etp'), may hold values from -0.109375 to 0.109375
Outputs:
- token_grad: bfloat16 [4096, 3584], P('ep')
- prob_grad: bfloat16 [4096, 2], P('ep')
- down_grad: bfloat16 [32, 3200, 3584], P('ep', 'etp')
The draws below stay inside these ranges and needn't reach their ends.
Inputs may be any that keep to these rules, and one draw needn't show every extreme that they name: `expert_ids`: each row names two different experts. Among the 128 rows of one device (aligned blocks of rows) no expert is named more than 16 times, and in every draw one expert is named exactly 16 times within the rows of every device.
All inputs are finite; a program needn't handle non-finite values.
Results may differ from the reference program's by a relative error of at most 0.02.
Values may be sent and summed in bfloat16 or wider, within the bound.
No kernel may reach another device: no remote copies, remote signals or barrier semaphores. Data moves between devices by JAX's collectives and lax.ppermute only.
A program may use at most 128 MiB of HBM per device.

```python
import jax
import jax.numpy as jnp
from jax import lax

D = 3584
FFE = 3200
TOP = 2
TOK_DEV = 128
EXPERTS = 32
CAP = 16
TOKENS = 4096
N_EP = 32
N_ETP = 8


def draw_expert_ids(key, part):
    key = jax.random.fold_in(key, 11)
    pop_key, hot_key, block_key = jax.random.split(key, 3)
    slot_total = EXPERTS * CAP
    favour = jax.random.randint(pop_key, (EXPERTS,), 0, 2 ** 14)
    hot_expert = jax.random.randint(hot_key, (), 0, EXPERTS)

    def one_block(block_index):
        inner_key = jax.random.fold_in(block_key, block_index)
        score_key, shuffle_key, swap_key = jax.random.split(inner_key, 3)
        slot_ids = jnp.arange(slot_total, dtype=jnp.int32)
        owners = slot_ids // CAP
        priority = jax.random.randint(score_key, (slot_total,), 0, 2 ** 14) + favour[owners]
        priority = priority + jnp.where(owners == 0, 2 ** 16, 0)
        priority = priority * slot_total + slot_ids
        ranking = jnp.argsort(-priority, stable=True)
        chosen = jnp.sort(ranking[:2 * TOK_DEV])
        picked = (chosen // CAP + hot_expert) % EXPERTS
        shuffle = jax.random.permutation(shuffle_key, TOK_DEV)
        first_col = picked[:TOK_DEV][shuffle]
        second_col = picked[TOK_DEV:][shuffle]
        swapped = jax.random.randint(swap_key, (TOK_DEV,), 0, 2) == 1
        return jnp.stack([jnp.where(swapped, second_col, first_col), jnp.where(swapped, first_col, second_col)], axis=1)
    blocks = lax.map(one_block, jnp.arange(N_EP, dtype=jnp.int32))
    return blocks.reshape(TOKENS, TOP).astype(jnp.int32)


def levels(rng, dims, pieces, least, high):
    level = 1.0
    for axis_at, blocks in pieces:
        steps = jax.random.uniform(jax.random.fold_in(jax.random.fold_in(rng, 6), axis_at), (blocks,), jnp.float32, least / len(pieces), high / len(pieces))
        level = level * jnp.repeat(jnp.exp(steps), dims[axis_at] // blocks).reshape((-1,) + (1,) * (len(dims) - 1 - axis_at))
    return level


def normal_values(stream_key, shape, deviation, most, shards=(), kind=jnp.bfloat16):
    entries = jax.random.normal(stream_key, shape, jnp.float32) * deviation
    if len(shards) > 0:
        entries = levels(stream_key, shape, shards, -0.22, 0.18) * entries
    return jnp.clip(entries, min=-most, max=most).astype(kind)


def setup_inputs(seed: int = 0) -> dict:
    keys = jax.random.split(jax.random.key(seed), 8)
    tokens = normal_values(keys[0], (TOKENS, D), 1.0, 6.0, ((0, 32),))
    out_grad = normal_values(keys[1], (TOKENS, D), 1.0, 6.0, ((0, 32),))
    expert_ids = draw_expert_ids(jax.random.fold_in(keys[7], 71), 0)
    route_probs = jnp.clip(0.099609375 + 0.9003906 * jax.random.uniform(keys[3], (TOKENS, TOP), jnp.float32) ** levels(keys[3], (TOKENS, TOP), ((0, 32),), -0.2, 0.2), 0.099609375, 1.0).astype(jnp.bfloat16)
    w_gate = normal_values(keys[4], (EXPERTS, D, FFE), D ** -0.5, 0.09375, ((0, 32), (2, 8)))
    w_up = normal_values(keys[5], (EXPERTS, D, FFE), D ** -0.5, 0.09375, ((0, 32), (2, 8)))
    w_down = normal_values(keys[6], (EXPERTS, FFE, D), FFE ** -0.5, 0.109375, ((0, 32), (1, 8)))
    return dict(tokens=tokens, out_grad=out_grad, expert_ids=expert_ids, route_probs=route_probs, w_gate=w_gate, w_up=w_up, w_down=w_down)


def reference(tokens, out_grad, expert_ids, route_probs, w_gate, w_up, w_down):
    route_count = TOKENS * TOP
    most_rows = N_EP * CAP
    block_width = FFE // N_ETP
    flat_ids = expert_ids.reshape(-1).astype(jnp.int32)
    flat_probs = route_probs.reshape(-1)
    sort_order = jnp.argsort(flat_ids, stable=True).astype(jnp.int32)
    sorted_ids = flat_ids[sort_order]
    counts = jnp.sum((flat_ids[:, None] == jnp.arange(EXPERTS, dtype=jnp.int32)[None, :]).astype(jnp.int32), axis=0)
    starts = (jnp.cumsum(counts) - counts).astype(jnp.int32)

    def one_expert(expert):
        sorted_pos = starts[expert] + jnp.arange(most_rows, dtype=jnp.int32)
        filled = jnp.arange(most_rows, dtype=jnp.int32) < counts[expert]
        route_index = sort_order[jnp.clip(sorted_pos, 0, route_count - 1)]
        token_index = route_index // TOP
        token_rows = jnp.where(filled[:, None], tokens[token_index], 0)
        grad_rows = jnp.where(filled[:, None], out_grad[token_index], 0)
        prob_rows = jnp.where(filled, flat_probs[route_index].astype(jnp.float32), 0.0)
        gate_matrix = w_gate[expert]
        up_matrix = w_up[expert]
        down_matrix = w_down[expert]
        gate_value = jnp.dot(token_rows, gate_matrix, preferred_element_type=jnp.float32)
        up_value = jnp.dot(token_rows, up_matrix, preferred_element_type=jnp.float32)
        gate_sigmoid = jax.nn.sigmoid(gate_value)
        hidden = (gate_value * gate_sigmoid * up_value).astype(jnp.bfloat16)
        hidden_grad = jnp.dot(grad_rows, down_matrix.T, preferred_element_type=jnp.float32)
        scaled_back = prob_rows[:, None] * hidden_grad
        up_grad = (scaled_back * gate_value * gate_sigmoid).astype(jnp.bfloat16)
        gate_grad = (scaled_back * up_value * gate_sigmoid * (1.0 + gate_value * (1.0 - gate_sigmoid))).astype(jnp.bfloat16)
        gate_blocks = gate_grad.astype(jnp.float32).reshape(most_rows, N_ETP, block_width)
        up_blocks = up_grad.astype(jnp.float32).reshape(most_rows, N_ETP, block_width)
        gate_weights = gate_matrix.astype(jnp.float32).reshape(D, N_ETP, block_width)
        up_weights = up_matrix.astype(jnp.float32).reshape(D, N_ETP, block_width)
        partial_value = jnp.einsum("rsf,dsf->srd", gate_blocks, gate_weights) + jnp.einsum("rsf,dsf->srd", up_blocks, up_weights)
        partial_value = lax.optimization_barrier(partial_value.astype(jnp.bfloat16))
        rows_grad = jnp.sum(partial_value.astype(jnp.float32), axis=0).astype(jnp.bfloat16)
        score_part = jnp.sum((hidden_grad * hidden.astype(jnp.float32)).reshape(most_rows, N_ETP, block_width), axis=2)
        score_part = lax.optimization_barrier(score_part.astype(jnp.bfloat16))
        score_total = jnp.sum(score_part.astype(jnp.float32), axis=1).astype(jnp.bfloat16)
        weighted_grad = (prob_rows[:, None] * grad_rows.astype(jnp.float32)).astype(jnp.bfloat16)
        down_block = jnp.dot(hidden.T, weighted_grad, preferred_element_type=jnp.float32).astype(jnp.bfloat16)
        return rows_grad, score_total, down_block

    rows_grad, score_total, down_grad = lax.map(one_expert, jnp.arange(EXPERTS, dtype=jnp.int32))
    position = jnp.arange(route_count, dtype=jnp.int32) - starts[sorted_ids]
    route_grad = jnp.zeros((route_count, D), jnp.bfloat16).at[sort_order].set(rows_grad[sorted_ids, position])
    route_score = jnp.zeros((route_count,), jnp.bfloat16).at[sort_order].set(score_total[sorted_ids, position])
    route_grad = route_grad.reshape(TOKENS, TOP, D)
    token_grad = (route_grad[:, 0].astype(jnp.float32) + route_grad[:, 1].astype(jnp.float32)).astype(jnp.bfloat16)
    prob_grad = route_score.reshape(TOKENS, TOP)
    return token_grad, prob_grad, down_grad
```

```python
import functools

import jax
import jax.numpy as jnp
from jax import lax
from jax.experimental import pallas as pl
from jax.experimental.pallas import tpu as pltpu
from jax.sharding import PartitionSpec as P

D = 3584
UNITS = 400
TOK = 128
EXPERTS = 32
N_Z = 8
ROWS = 256
QUARTER = D // 4
WIDE = 384
PACK = 2 * WIDE + 128
BF = jnp.bfloat16
F32 = jnp.float32
VMEM_BYTES = 56 * 2**20

NT = (((1,), (1,)), ((), ()))
TN = (((0,), (0,)), ((), ()))
NN = (((1,), (0,)), ((), ()))


def mm(left, right, dims=NN):
    return lax.dot_general(left, right, dims, preferred_element_type=F32)


def params():
    return pltpu.CompilerParams(vmem_limit_bytes=VMEM_BYTES)


VM = pl.BlockSpec(memory_space=pltpu.VMEM)
SM = pl.BlockSpec(memory_space=pltpu.SMEM)
ANY = pl.BlockSpec(memory_space=pl.ANY)


def slots_of(ids_ref):
    expert = lax.broadcasted_iota(jnp.int32, (EXPERTS, TOK), 0)
    first = ids_ref[0:1, :]
    second = ids_ref[1:2, :]
    hot0 = (expert == first).astype(F32)
    hot1 = (expert == second).astype(F32)
    earlier = lax.broadcasted_iota(jnp.int32, (TOK, TOK), 0) < lax.broadcasted_iota(
        jnp.int32, (TOK, TOK), 1
    )
    before = earlier.astype(BF)
    rank0 = mm(hot0.astype(BF), before)
    rank1 = mm(hot1.astype(BF), before) + jnp.sum(hot0, axis=1, keepdims=True)
    pos0 = jnp.sum(hot0 * rank0, axis=0, keepdims=True).astype(jnp.int32)
    pos1 = jnp.sum(hot1 * rank1, axis=0, keepdims=True).astype(jnp.int32)
    return first * 16 + pos0, second * 16 + pos1


def row_hot(slot, half):
    row = lax.broadcasted_iota(jnp.int32, (ROWS, TOK), 0)
    return ((row >> 3) * 16 + half * 8 + (row & 7)) == slot


def send_tokens_kernel(z_ref, ids_ref, tok_ref, out_ref):
    z = z_ref[0]
    slot0, slot1 = slots_of(ids_ref)
    half = z // 4
    hot = jnp.logical_or(row_hot(slot0, half), row_hot(slot1, half)).astype(BF)
    cols = pl.ds(pl.multiple_of((z % 4) * QUARTER, 128), QUARTER)
    out_ref[...] = mm(hot, tok_ref[:, cols]).astype(BF)


def send_grads_kernel(ids_ref, prob_ref, grad_ref, out0_ref, out1_ref):
    slot0, slot1 = slots_of(ids_ref)
    p0 = prob_ref[0:1, :].astype(F32)
    p1 = prob_ref[1:2, :].astype(F32)
    for half, out_ref in ((0, out0_ref), (1, out1_ref)):
        hot0 = row_hot(slot0, half)
        hot1 = row_hot(slot1, half)
        hot = jnp.logical_or(hot0, hot1).astype(BF)
        prob = jnp.sum(
            jnp.where(hot0, p0, 0.0) + jnp.where(hot1, p1, 0.0), axis=1, keepdims=True
        )
        for c in range(0, D, QUARTER):
            out_ref[:, c : c + QUARTER] = (
                mm(hot, grad_ref[:, c : c + QUARTER]) * prob
            ).astype(BF)


def gate_up_kernel(offsets, z_ref, *refs):
    xs = refs[:8]
    gate_w, up_w = refs[8:10]
    outs = refs[10:14]
    x_buf, wg_buf, wu_buf, sems = refs[14:]
    z = z_ref[0]
    copies = [
        pltpu.make_async_copy(gate_w, wg_buf, sems.at[8]),
        pltpu.make_async_copy(up_w, wu_buf, sems.at[9]),
    ]
    for i, off in enumerate(offsets):
        owner = lax.rem(z + off + 8, 8)
        cols = pl.ds(pl.multiple_of(lax.rem(owner, 4) * QUARTER, 128), QUARTER)
        copies.append(
            pltpu.make_async_copy(xs[i], x_buf.at[owner // 4, :, cols], sems.at[i])
        )
    for c in copies:
        c.start()
    for c in copies:
        c.wait()
    for half in range(2):
        outs[2 * half][...] = mm(x_buf[half], wg_buf[...], NT)
        outs[2 * half + 1][...] = mm(x_buf[half], wu_buf[...], NT)


def expert_kernel(
    z_ref, rows_hbm, down_w, gate_w, up_w, gate_ref, up_ref, *refs
):
    packs = refs[:8]
    score_ref, hid_ref, rows, wd, wg, wu, part, sems = refs[8:]
    z = z_ref[0]
    c_rows = pltpu.make_async_copy(rows_hbm, rows, sems.at[0])
    c_wd = pltpu.make_async_copy(down_w, wd, sems.at[1])
    c_wg = pltpu.make_async_copy(gate_w, wg, sems.at[2])
    c_wu = pltpu.make_async_copy(up_w, wu, sems.at[3])
    for c in (c_rows, c_wd, c_wg, c_wu):
        c.start()
    c_rows.wait()
    c_wd.wait()
    back = mm(rows[...], wd[...], NT)
    gate = gate_ref[...]
    up = up_ref[...]
    sig = jax.nn.sigmoid(gate)
    hidden = (gate * sig * up).astype(BF)
    hid_ref[...] = hidden
    up_grad = (back * gate * sig).astype(BF)
    gate_grad = (back * up * sig * (1.0 + gate * (1.0 - sig))).astype(BF)
    score = jnp.sum(back * hidden.astype(F32), axis=1, keepdims=True)
    score_ref[...] = jnp.broadcast_to(score, (ROWS, 128)).astype(BF)
    c_wg.wait()
    c_wu.wait()
    for c in range(0, D, QUARTER):
        part[:, c : c + QUARTER] = (
            mm(gate_grad, wg[:, c : c + QUARTER]) + mm(up_grad, wu[:, c : c + QUARTER])
        ).astype(BF)
    lane = lax.broadcasted_iota(jnp.int32, (128, 128), 1)
    for r in range(8):
        shard = lax.rem(z + r, 8)
        cols = pl.ds(pl.multiple_of(shard * WIDE, 128), WIDE)
        tile = pl.ds(pl.multiple_of((24 + shard // 2) * 128, 128), 128)
        packs[r][:, :WIDE] = part[0:128, cols]
        packs[r][:, WIDE : 2 * WIDE] = part[128:256, cols]
        top = part[0:128, tile].astype(F32)
        bottom = part[128:256, tile].astype(F32)
        odd = lax.rem(shard, 2) == 1
        top = jnp.where(odd, pltpu.roll(top, 64, 1), top)
        bottom = jnp.where(odd, bottom, pltpu.roll(bottom, 64, 1))
        packs[r][:, 2 * WIDE :] = jnp.where(lane < 64, top, bottom).astype(BF)


def back_kernel(*refs):
    out_ref = refs[8]
    lane = lax.broadcasted_iota(jnp.int32, (128, 128), 1)
    tiles = []
    for half in range(2):
        own, left, right = refs[3 * half : 3 * half + 3]
        total = (
            own[...].astype(F32) + left[...].astype(F32) + right[...].astype(F32)
        )
        base = half * WIDE
        out_ref[0:128, base : base + WIDE] = total[:, :WIDE].astype(BF)
        out_ref[128:256, base : base + WIDE] = total[:, WIDE : 2 * WIDE].astype(BF)
        tile = total[:, 2 * WIDE :]
        tiles.append((tile, pltpu.roll(tile, 64, 1)))
    (t0, r0), (t1, r1) = tiles
    out_ref[0:128, 2 * WIDE : PACK] = jnp.where(lane < 64, t0, r1).astype(BF)
    out_ref[128:256, 2 * WIDE : PACK] = jnp.where(lane < 64, r0, t1).astype(BF)
    score0, score1 = refs[6], refs[7]
    wide = lax.broadcasted_iota(jnp.int32, (ROWS, 128), 1)
    out_ref[:, PACK:] = jnp.where(
        wide == 0, score0[...].astype(F32), jnp.where(wide == 1, score1[...].astype(F32), 0.0)
    ).astype(BF)


def token_sum_kernel(ids_ref, got_ref, out_ref):
    slot0, slot1 = slots_of(ids_ref)
    hots = [
        [row_hot(slot, half).astype(BF) for slot in (slot0, slot1)] for half in range(2)
    ]
    both = [h[0] + h[1] for h in hots]
    out_ref[:, :WIDE] = (
        mm(both[0], got_ref[:, :WIDE], TN) + mm(both[1], got_ref[:, WIDE : 2 * WIDE], TN)
    ).astype(BF)
    tile = got_ref[:, 2 * WIDE : PACK]
    low = mm(both[0], tile, TN)
    high = pltpu.roll(mm(both[1], tile, TN), 64, 1)
    scores = got_ref[:, PACK:]
    lane = lax.broadcasted_iota(jnp.int32, (128, 128), 1)
    result = jnp.where(lane < 64, low + high, 0.0)
    for k in range(2):
        total = mm(hots[0][k], scores, TN)[:, 0:1] + mm(hots[1][k], scores, TN)[:, 1:2]
        result = jnp.where(lane == 64 + k, total, result)
    out_ref[:, WIDE:] = result.astype(BF)


def assemble_kernel(offsets, z_ref, *refs):
    shards = refs[:8]
    out_ref, prob_ref, tiles = refs[8:]
    z = z_ref[0]
    total = jnp.zeros((128, 128), F32)
    for i, off in enumerate(offsets):
        owner = lax.rem(z + off + 8, 8)
        cols = pl.ds(pl.multiple_of(owner * WIDE, 128), WIDE)
        out_ref[:, cols] = shards[i][:, :WIDE]
        tile = shards[i][:, WIDE:].astype(F32)
        tiles[owner] = tile
        total = total + tile
    prob_ref[...] = total
    lane = lax.broadcasted_iota(jnp.int32, (128, 128), 1)
    for j in range(4):
        c = 8 * WIDE + 128 * j
        out_ref[:, c : c + 128] = jnp.where(
            lane < 64, tiles[2 * j], pltpu.roll(tiles[2 * j + 1], 64, 1)
        ).astype(BF)


def down_kernel(hid0, hid1, rows0, rows1, out_ref):
    out_ref[...] = (
        mm(hid0[...], rows0[...], TN) + mm(hid1[...], rows1[...], TN)
    ).astype(BF)


RIGHT = [(i, (i + 1) % N_Z) for i in range(N_Z)]
LEFT = [(i, (i - 1) % N_Z) for i in range(N_Z)]
OFFSETS = (0, -1, 1, -2, 2, -3, 3, -4)


def to_right(x):
    return lax.ppermute(x, "etp", RIGHT)


def to_left(x):
    return lax.ppermute(x, "etp", LEFT)


def ring_gather(x):
    shards = [x]
    from_left = from_right = x
    for step in range(4):
        from_left = to_right(from_left)
        shards.append(from_left)
        if step < 3:
            from_right = to_left(from_right)
            shards.append(from_right)
    return shards


def add_rows(a, b):
    return (a.astype(F32) + b.astype(F32)).astype(BF)


def ring_scatter(packs):
    from_left = to_right(packs[4])
    from_right = to_left(packs[5])
    for step in range(3):
        from_left = to_right(add_rows(from_left, packs[3 - step]))
        if step < 2:
            from_right = to_left(add_rows(from_right, packs[6 + step]))
    return from_left, from_right


def exchange(x):
    return lax.all_to_all(x, "ep", split_axis=0, concat_axis=0, tiled=True)


def shape(*dims, dtype=BF):
    return jax.ShapeDtypeStruct(dims, dtype)


def on_device(tokens, out_grad, expert_ids, route_probs, w_gate, w_up, w_down):
    z = lax.axis_index("etp").astype(jnp.int32).reshape(1)
    ids = expert_ids.T
    probs = route_probs.T
    gate_w = w_gate[0].T
    up_w = w_up[0].T
    down_w = w_down[0]

    send_x = pl.pallas_call(
        send_tokens_kernel,
        out_shape=shape(ROWS, QUARTER),
        in_specs=[SM, VM, VM],
        out_specs=VM,
        compiler_params=params(),
        name="send_tokens",
    )(z, ids, tokens)
    got_x = exchange(send_x.reshape(EXPERTS, 8, QUARTER)).reshape(ROWS, QUARTER)
    send_g = pl.pallas_call(
        send_grads_kernel,
        out_shape=[shape(ROWS, D)] * 2,
        in_specs=[VM] * 3,
        out_specs=[VM] * 2,
        compiler_params=params(),
        name="send_grads",
    )(ids, probs, out_grad)
    rows = [exchange(g.reshape(EXPERTS, 8, D)).reshape(ROWS, D) for g in send_g]

    gate_up = pl.pallas_call(
        functools.partial(gate_up_kernel, OFFSETS),
        out_shape=[shape(ROWS, UNITS, dtype=F32)] * 4,
        in_specs=[SM] + [ANY] * 10,
        out_specs=[VM] * 4,
        scratch_shapes=[
            pltpu.VMEM((2, ROWS, D), BF),
            pltpu.VMEM((UNITS, D), BF),
            pltpu.VMEM((UNITS, D), BF),
            pltpu.SemaphoreType.DMA((10,)),
        ],
        compiler_params=params(),
        name="gate_up",
    )(z, *ring_gather(got_x), gate_w, up_w)

    back_parts = []
    scores = []
    hiddens = []
    for half in range(2):
        *packs, score, hidden = pl.pallas_call(
            expert_kernel,
            out_shape=[shape(128, PACK)] * 8 + [shape(ROWS, 128), shape(ROWS, UNITS)],
            in_specs=[SM] + [ANY] * 4 + [VM] * 2,
            out_specs=[VM] * 10,
            scratch_shapes=[
                pltpu.VMEM((ROWS, D), BF),
                pltpu.VMEM((UNITS, D), BF),
                pltpu.VMEM((UNITS, D), BF),
                pltpu.VMEM((UNITS, D), BF),
                pltpu.VMEM((ROWS, D), BF),
                pltpu.SemaphoreType.DMA((4,)),
            ],
            compiler_params=params(),
            name="expert",
        )(z, rows[half], down_w, gate_w, up_w, *gate_up[2 * half : 2 * half + 2])
        back_parts += [packs[0], *ring_scatter(packs)]
        scores.append(score)
        hiddens.append(hidden)

    send_back = pl.pallas_call(
        back_kernel,
        out_shape=shape(ROWS, PACK + 128),
        in_specs=[VM] * 8,
        out_specs=VM,
        compiler_params=params(),
        name="pack_back",
    )(*back_parts, *scores)
    got_back = exchange(send_back.reshape(EXPERTS, 8, PACK + 128)).reshape(ROWS, PACK + 128)
    summed = pl.pallas_call(
        token_sum_kernel,
        out_shape=shape(TOK, 512),
        in_specs=[VM] * 2,
        out_specs=VM,
        compiler_params=params(),
        name="token_sum",
    )(ids, got_back)
    token_grad, prob_total = pl.pallas_call(
        functools.partial(assemble_kernel, OFFSETS),
        out_shape=[shape(TOK, D), shape(128, 128, dtype=F32)],
        in_specs=[SM] + [VM] * 8,
        out_specs=[VM] * 2,
        scratch_shapes=[pltpu.VMEM((8, 128, 128), F32)],
        compiler_params=params(),
        name="assemble",
    )(z, *ring_gather(summed))
    prob_grad = (prob_total[:, 64:66] / route_probs.astype(F32)).astype(BF)

    block = 512
    down_grad = pl.pallas_call(
        down_kernel,
        out_shape=shape(UNITS, D),
        grid=(D // block,),
        in_specs=[pl.BlockSpec((ROWS, UNITS), lambda i: (0, 0))] * 2
        + [pl.BlockSpec((ROWS, block), lambda i: (0, i))] * 2,
        out_specs=pl.BlockSpec((UNITS, block), lambda i: (0, i)),
        compiler_params=params(),
        name="down_grad",
    )(*hiddens, *rows)
    return (token_grad, prob_grad, down_grad[None])


def solution(mesh):
    return jax.shard_map(
        on_device,
        mesh=mesh,
        in_specs=(
            P("ep", None),
            P("ep", None),
            P("ep", None),
            P("ep", None),
            P("ep", None, "etp"),
            P("ep", None, "etp"),
            P("ep", "etp", None),
        ),
        out_specs=(P("ep", None), P("ep", None), P("ep", "etp", None)),
        check_vma=False,
    )
```

```python
import functools

import jax
import jax.numpy as jnp
from jax import lax
from jax.experimental import pallas as pl
from jax.experimental.pallas import tpu as pltpu
from jax.sharding import PartitionSpec as P

D = 3584
UNITS = 400
TOK = 128
EXPERTS = 32
N_Z = 8
ROWS = 256
QUARTER = D // 4
WIDE = 384
PACK = 2 * WIDE + 128
BF = jnp.bfloat16
F32 = jnp.float32

NT = (((1,), (1,)), ((), ()))
TN = (((0,), (0,)), ((), ()))
NN = (((1,), (0,)), ((), ()))


def mm(left, right, dims=NN):
    return lax.dot_general(left, right, dims, preferred_element_type=F32)


def params(mib=20):
    return pltpu.CompilerParams(vmem_limit_bytes=mib * 2**20)


VM = pl.BlockSpec(memory_space=pltpu.VMEM)
SM = pl.BlockSpec(memory_space=pltpu.SMEM)
HBM = pl.BlockSpec(memory_space=pltpu.HBM)


def slots_of(ids_ref):
    expert = lax.broadcasted_iota(jnp.int32, (EXPERTS, TOK), 0)
    first = ids_ref[0:1, :]
    second = ids_ref[1:2, :]
    hot0 = (expert == first).astype(F32)
    hot1 = (expert == second).astype(F32)
    earlier = lax.broadcasted_iota(jnp.int32, (TOK, TOK), 0) < lax.broadcasted_iota(
        jnp.int32, (TOK, TOK), 1
    )
    before = earlier.astype(BF)
    rank0 = mm(hot0.astype(BF), before)
    rank1 = mm(hot1.astype(BF), before) + jnp.sum(hot0, axis=1, keepdims=True)
    pos0 = jnp.sum(hot0 * rank0, axis=0, keepdims=True).astype(jnp.int32)
    pos1 = jnp.sum(hot1 * rank1, axis=0, keepdims=True).astype(jnp.int32)
    return first * 16 + pos0, second * 16 + pos1


def row_hot(slot, half):
    row = lax.broadcasted_iota(jnp.int32, (ROWS, TOK), 0)
    return ((row >> 3) * 16 + half * 8 + (row & 7)) == slot


def hot_of(slots, half):
    return jnp.logical_or(row_hot(slots[0], half), row_hot(slots[1], half)).astype(BF)


def prob_of(slots, prob_ref, half):
    weight = jnp.zeros((ROWS, TOK), F32)
    for k in range(2):
        weight += jnp.where(row_hot(slots[k], half), prob_ref[k : k + 1, :].astype(F32), 0.0)
    return jnp.sum(weight, axis=1, keepdims=True)


def send_ring_kernel(
    z_ref, ids_hbm, prob_hbm, tok_hbm, grad_hbm, out_ref, ids_ref, prob_ref, buf, sems
):
    z = z_ref[0]
    c_ids = pltpu.make_async_copy(ids_hbm, ids_ref, sems.at[0])
    c_prob = pltpu.make_async_copy(prob_hbm, prob_ref, sems.at[1])
    c_ids.start()
    c_prob.start()
    cols = pl.ds(pl.multiple_of(lax.rem(z, 4) * QUARTER, 128), QUARTER)
    of_tokens = pltpu.make_async_copy(tok_hbm.at[:, cols], buf, sems.at[2])
    of_grads = pltpu.make_async_copy(grad_hbm.at[:, cols], buf, sems.at[2])

    @pl.when(z < 4)
    def _():
        of_tokens.start()

    @pl.when(z >= 4)
    def _():
        of_grads.start()

    c_ids.wait()
    slots = slots_of(ids_ref)
    hot = hot_of(slots, 0)
    c_prob.wait()
    prob = jnp.where(z < 4, 1.0, prob_of(slots, prob_ref, 0))
    of_tokens.wait()
    out_ref[...] = (mm(hot, buf[...]) * prob).astype(BF)


def send_plane_kernel(
    ids_hbm, prob_hbm, tok_hbm, grad_hbm, out_ref, ids_ref, prob_ref, tok_ref, grad_ref, sems
):
    copies = [
        pltpu.make_async_copy(src, dst, sems.at[i])
        for i, (src, dst) in enumerate(
            ((ids_hbm, ids_ref), (prob_hbm, prob_ref), (tok_hbm, tok_ref), (grad_hbm, grad_ref))
        )
    ]
    for c in copies:
        c.start()
    copies[0].wait()
    slots = slots_of(ids_ref)
    hot = hot_of(slots, 1)
    copies[1].wait()
    prob = prob_of(slots, prob_ref, 1)
    copies[2].wait()
    copies[3].wait()
    for c in range(0, D, QUARTER):
        out_ref[:, c : c + QUARTER] = mm(hot, tok_ref[:, c : c + QUARTER]).astype(BF)
        out_ref[:, D + c : D + c + QUARTER] = (
            mm(hot, grad_ref[:, c : c + QUARTER]) * prob
        ).astype(BF)


def quarter(q):
    return pl.ds(q * QUARTER, QUARTER)


def expert_kernel(from_ring, z_ref, *refs):
    n = 16 if from_ring else 1
    sources, refs = refs[:n], refs[n:]
    down_hbm, gate_hbm, up_hbm = refs[:3]
    packs = refs[3:11]
    score_ref, hid_ref, rows_hbm = refs[11:14]
    rows, down_w, gate_w, up_w, part, row_sems, sems, out_sem = refs[14:]
    z = z_ref[0]
    row_waits = [[] for _ in range(8)]
    row_starts = []
    if from_ring:
        for chain, offsets in enumerate(OFFSETS):
            here = pl.ds(chain * 128, 128)
            for i, off in enumerate(offsets):
                owner = lax.rem(z + off + 8, 8)
                cols = pl.ds(pl.multiple_of(lax.rem(owner, 4) * QUARTER, 128), QUARTER)
                source = sources[8 * chain + i]
                row_starts.append(
                    pltpu.make_async_copy(
                        source, rows.at[owner // 4, here, cols], row_sems.at[chain, owner]
                    )
                )
                row_waits[i].append(
                    pltpu.make_async_copy(
                        source, rows.at[i // 4, here, quarter(i % 4)], row_sems.at[chain, i]
                    )
                )
    else:
        for i in range(8):
            c = pltpu.make_async_copy(
                sources[0].at[:, quarter(i)], rows.at[i // 4, :, quarter(i % 4)], row_sems.at[0, i]
            )
            row_starts.append(c)
            row_waits[i].append(c)
    weights = [
        [
            pltpu.make_async_copy(src.at[:, quarter(q)], dst.at[:, quarter(q)], sems.at[k, q])
            for q in range(4)
        ]
        for k, (src, dst) in enumerate(
            ((gate_hbm, gate_w), (up_hbm, up_w), (down_hbm, down_w))
        )
    ]
    if from_ring:
        for c in row_starts:
            c.start()
    for q in range(4):
        if not from_ring:
            row_starts[q].start()
        weights[0][q].start()
        weights[1][q].start()
    for q in range(4):
        if not from_ring:
            row_starts[4 + q].start()
        weights[2][q].start()
    gate = up = back = 0.0
    for q in range(0, 4, 2):
        for p in (q, q + 1):
            for c in (*row_waits[p], weights[0][p], weights[1][p]):
                c.wait()
        cols = slice(q * QUARTER, (q + 2) * QUARTER)
        gate = gate + mm(rows[0, :, cols], gate_w[:, cols], NT)
        up = up + mm(rows[0, :, cols], up_w[:, cols], NT)
    for q in range(0, 4, 2):
        for p in (q, q + 1):
            for c in (*row_waits[4 + p], weights[2][p]):
                c.wait()
        cols = slice(q * QUARTER, (q + 2) * QUARTER)
        back = back + mm(rows[1, :, cols], down_w[:, cols], NT)
    if from_ring:
        rows_out = pltpu.make_async_copy(rows.at[1], rows_hbm, out_sem)
        rows_out.start()
    sig = jax.nn.sigmoid(gate)
    hidden = (gate * sig * up).astype(BF)
    hid_ref[...] = hidden
    up_grad = (back * gate * sig).astype(BF)
    gate_grad = (back * up * sig * (1.0 + gate * (1.0 - sig))).astype(BF)
    score = jnp.sum(back * hidden.astype(F32), axis=1, keepdims=True)
    score_ref[...] = jnp.broadcast_to(score, (ROWS, 128)).astype(BF)
    for c in range(0, D, QUARTER):
        part[:, c : c + QUARTER] = (
            mm(gate_grad, gate_w[:, c : c + QUARTER]) + mm(up_grad, up_w[:, c : c + QUARTER])
        ).astype(BF)
    lane = lax.broadcasted_iota(jnp.int32, (128, 128), 1)
    for r in range(8):
        shard = lax.rem(z + r, 8)
        cols = pl.ds(pl.multiple_of(shard * WIDE, 128), WIDE)
        tile = pl.ds(pl.multiple_of((24 + shard // 2) * 128, 128), 128)
        odd = lax.rem(shard, 2) == 1
        packs[r][:, :WIDE] = part[0:128, cols]
        packs[r][:, WIDE : 2 * WIDE] = part[128:256, cols]
        top = part[0:128, tile].astype(F32)
        bottom = part[128:256, tile].astype(F32)
        top = jnp.where(odd, pltpu.roll(top, 64, 1), top)
        bottom = jnp.where(odd, bottom, pltpu.roll(bottom, 64, 1))
        packs[r][:, 2 * WIDE :] = jnp.where(lane < 64, top, bottom).astype(BF)
    if from_ring:
        rows_out.wait()


def back_kernel(*refs):
    out_ref = refs[8]
    lane = lax.broadcasted_iota(jnp.int32, (128, 128), 1)
    tiles = []
    for half in range(2):
        own, left, right = refs[3 * half : 3 * half + 3]
        total = (
            own[...].astype(F32) + left[...].astype(F32) + right[...].astype(F32)
        )
        base = half * WIDE
        out_ref[0:128, base : base + WIDE] = total[:, :WIDE].astype(BF)
        out_ref[128:256, base : base + WIDE] = total[:, WIDE : 2 * WIDE].astype(BF)
        tile = total[:, 2 * WIDE :]
        tiles.append((tile, pltpu.roll(tile, 64, 1)))
    (t0, r0), (t1, r1) = tiles
    out_ref[0:128, 2 * WIDE : PACK] = jnp.where(lane < 64, t0, r1).astype(BF)
    out_ref[128:256, 2 * WIDE : PACK] = jnp.where(lane < 64, r0, t1).astype(BF)
    score0, score1 = refs[6][...], refs[7][...]
    wide = lax.broadcasted_iota(jnp.int32, (ROWS, 128), 1)
    out_ref[:, PACK:] = jnp.where(
        wide == 0, score0.astype(F32), jnp.where(wide == 1, score1.astype(F32), 0.0)
    ).astype(BF)


def token_sum_kernel(ids_ref, got_ref, out_ref):
    slot0, slot1 = slots_of(ids_ref)
    hots = [
        [row_hot(slot, half).astype(BF) for slot in (slot0, slot1)] for half in range(2)
    ]
    both = [h[0] + h[1] for h in hots]
    out_ref[:, :WIDE] = (
        mm(both[0], got_ref[:, :WIDE], TN) + mm(both[1], got_ref[:, WIDE : 2 * WIDE], TN)
    ).astype(BF)
    tile = got_ref[:, 2 * WIDE : PACK]
    low = mm(both[0], tile, TN)
    high = pltpu.roll(mm(both[1], tile, TN), 64, 1)
    scores = got_ref[:, PACK:]
    lane = lax.broadcasted_iota(jnp.int32, (128, 128), 1)
    result = jnp.where(lane < 64, low + high, 0.0)
    for k in range(2):
        total = mm(hots[0][k], scores, TN)[:, 0:1] + mm(hots[1][k], scores, TN)[:, 1:2]
        result = jnp.where(lane == 64 + k, total, result)
    out_ref[:, WIDE:] = result.astype(BF)


def assemble_kernel(offsets, z_ref, prob_in, *refs):
    shards = refs[:8]
    out_ref, prob_ref, tiles = refs[8:]
    z = z_ref[0]
    total = jnp.zeros((128, 128), F32)
    for i, off in enumerate(offsets):
        owner = lax.rem(z + off + 8, 8)
        cols = pl.ds(pl.multiple_of(owner * WIDE, 128), WIDE)
        out_ref[:, cols] = shards[i][:, :WIDE]
        tile = shards[i][:, WIDE:].astype(F32)
        tiles[owner] = tile
        total = total + tile
    prob_ref[...] = (total.T[64:66, :] / prob_in[...].astype(F32)).astype(BF)
    lane = lax.broadcasted_iota(jnp.int32, (128, 128), 1)
    for j in range(4):
        c = 8 * WIDE + 128 * j
        out_ref[:, c : c + 128] = jnp.where(
            lane < 64, tiles[2 * j], pltpu.roll(tiles[2 * j + 1], 64, 1)
        ).astype(BF)


def down_kernel(hid0, hid1, rows0, rows1, out_ref):
    out_ref[...] = (
        mm(hid0[...], rows0[...], TN) + mm(hid1[...], rows1[...], TN)
    ).astype(BF)


OFFSETS = ((0, -1, 1, -2, 2, -3, 3, -4), (0, 1, -1, 2, -2, 3, -3, 4))


def hop(x, by):
    return lax.ppermute(x, "etp", [(i, (i + by) % N_Z) for i in range(N_Z)])


def ring_gather(x, way):
    shards = [x]
    far = near = x
    for step in range(4):
        far = hop(far, way)
        shards.append(far)
        if step < 3:
            near = hop(near, -way)
            shards.append(near)
    return shards


def add_rows(a, b):
    return (a.astype(F32) + b.astype(F32)).astype(BF)


def ring_scatter(packs, sums, way):
    far, near = sums
    for step in range(3):
        far = hop(add_rows(far, packs[4 - way * (step + 1)]), way)
        if step < 2:
            near = hop(add_rows(near, packs[4 + way * (step + 2)]), -way)
    return far, near


def exchange(x):
    return lax.all_to_all(x, "ep", split_axis=0, concat_axis=0, tiled=True)


def shape(*dims, dtype=BF):
    return jax.ShapeDtypeStruct(dims, dtype)


def on_device(tokens, out_grad, expert_ids, route_probs, w_gate, w_up, w_down):
    z = lax.axis_index("etp").astype(jnp.int32).reshape(1)
    ids = expert_ids.T
    probs = route_probs.T
    gate_w = w_gate[0].T
    up_w = w_up[0].T
    down_w = w_down[0]

    small = [
        pltpu.VMEM((2, TOK), jnp.int32),
        pltpu.VMEM((2, TOK), BF),
    ]
    send_ring = pl.pallas_call(
        send_ring_kernel,
        out_shape=shape(ROWS, QUARTER),
        in_specs=[SM] + [HBM] * 4,
        out_specs=VM,
        scratch_shapes=small + [pltpu.VMEM((TOK, QUARTER), BF), pltpu.SemaphoreType.DMA((3,))],
        compiler_params=params(60),
        name="send_ring",
    )(z, ids, probs, tokens, out_grad)
    got_ring = exchange(send_ring.reshape(EXPERTS, 8, QUARTER)).reshape(ROWS, QUARTER)
    send_plane = pl.pallas_call(
        send_plane_kernel,
        out_shape=shape(ROWS, 2 * D),
        in_specs=[HBM] * 4,
        out_specs=VM,
        scratch_shapes=small
        + [pltpu.VMEM((TOK, D), BF)] * 2
        + [pltpu.SemaphoreType.DMA((4,))],
        compiler_params=params(60),
        name="send_plane",
    )(ids, probs, tokens, out_grad)
    got_plane = exchange(send_plane.reshape(EXPERTS, 8, 2 * D)).reshape(ROWS, 2 * D)
    chains = ring_gather(got_ring[:128], 1) + ring_gather(got_ring[128:], -1)

    def expert(from_ring, sources):
        return pl.pallas_call(
            functools.partial(expert_kernel, from_ring),
            out_shape=[shape(128, PACK)] * 8
            + [shape(ROWS, 128), shape(ROWS, UNITS), shape(ROWS, D if from_ring else 128)],
            in_specs=[SM] + [HBM] * (len(sources) + 3),
            out_specs=[VM] * 10 + [HBM],
            scratch_shapes=[pltpu.VMEM((2, ROWS, D), BF)]
            + [pltpu.VMEM((UNITS, D), BF)] * 3
            + [
                pltpu.VMEM((ROWS, D), BF),
                pltpu.SemaphoreType.DMA((2, 8)),
                pltpu.SemaphoreType.DMA((3, 4)),
                pltpu.SemaphoreType.DMA(()),
            ],
            compiler_params=params(60),
            name="ring_expert" if from_ring else "plane_expert",
        )(z, *sources, down_w, gate_w, up_w)

    *packs0, score0, hidden0, ring_rows = expert(True, chains)
    sums0 = (hop(packs0[4], 1), hop(packs0[5], -1))
    *packs1, score1, hidden1, _ = expert(False, [got_plane])
    sums0, packs1 = lax.optimization_barrier((sums0, packs1))
    sums1 = (hop(packs1[4], -1), hop(packs1[3], 1))
    back_parts = [
        packs0[0],
        *ring_scatter(packs0, sums0, 1),
        packs1[0],
        *ring_scatter(packs1, sums1, -1),
        score0,
        score1,
    ]

    send_back = pl.pallas_call(
        back_kernel,
        out_shape=shape(ROWS, PACK + 128),
        in_specs=[VM] * 8,
        out_specs=VM,
        compiler_params=params(),
        name="pack_back",
    )(*back_parts)
    got_back = exchange(send_back.reshape(EXPERTS, 8, PACK + 128)).reshape(ROWS, PACK + 128)
    summed = pl.pallas_call(
        token_sum_kernel,
        out_shape=shape(TOK, 512),
        in_specs=[VM] * 2,
        out_specs=VM,
        compiler_params=params(),
        name="token_sum",
    )(ids, got_back)
    token_grad, prob_grad = pl.pallas_call(
        functools.partial(assemble_kernel, OFFSETS[0]),
        out_shape=[shape(TOK, D), shape(2, TOK)],
        in_specs=[SM] + [VM] * 9,
        out_specs=[VM] * 2,
        scratch_shapes=[pltpu.VMEM((8, 128, 128), F32)],
        compiler_params=params(),
        name="assemble",
    )(z, probs, *ring_gather(summed, 1))

    down_grad = pl.pallas_call(
        down_kernel,
        out_shape=shape(UNITS, D),
        grid=(4,),
        in_specs=[
            pl.BlockSpec((ROWS, UNITS), lambda i: (0, 0)),
            pl.BlockSpec((ROWS, UNITS), lambda i: (0, 0)),
            pl.BlockSpec((ROWS, QUARTER), lambda i: (0, i)),
            pl.BlockSpec((ROWS, QUARTER), lambda i: (0, 4 + i)),
        ],
        out_specs=pl.BlockSpec((UNITS, QUARTER), lambda i: (0, i)),
        compiler_params=params(),
        name="down_grad",
    )(hidden0, hidden1, ring_rows, got_plane)
    return (token_grad, prob_grad.T, down_grad[None])


def solution(mesh):
    return jax.shard_map(
        on_device,
        mesh=mesh,
        in_specs=(
            P("ep", None),
            P("ep", None),
            P("ep", None),
            P("ep", None),
            P("ep", None, "etp"),
            P("ep", None, "etp"),
            P("ep", "etp", None),
        ),
        out_specs=(P("ep", None), P("ep", None), P("ep", "etp", None)),
        check_vma=False,
    )
```

```python
import functools

import jax
import jax.numpy as jnp
from jax import lax
from jax.experimental import pallas as pl
from jax.experimental.pallas import tpu as pltpu
from jax.sharding import PartitionSpec as P

D = 3584
UNITS = 400
TOK = 128
EXPERTS = 32
N_Z = 8
ROWS = 256
QUARTER = D // 4
WIDE = 384
PACK = 2 * WIDE + 128
BF = jnp.bfloat16
F32 = jnp.float32

NT = (((1,), (1,)), ((), ()))
TN = (((0,), (0,)), ((), ()))
NN = (((1,), (0,)), ((), ()))


def mm(left, right, dims=NN):
    return lax.dot_general(left, right, dims, preferred_element_type=F32)


def params(mib=20):
    return pltpu.CompilerParams(vmem_limit_bytes=mib * 2**20)


VM = pl.BlockSpec(memory_space=pltpu.VMEM)
SM = pl.BlockSpec(memory_space=pltpu.SMEM)
HBM = pl.BlockSpec(memory_space=pltpu.HBM)


def slots_of(ids_ref):
    expert = lax.broadcasted_iota(jnp.int32, (EXPERTS, TOK), 0)
    first = ids_ref[0:1, :]
    second = ids_ref[1:2, :]
    hot0 = (expert == first).astype(F32)
    hot1 = (expert == second).astype(F32)
    earlier = lax.broadcasted_iota(jnp.int32, (TOK, TOK), 0) < lax.broadcasted_iota(
        jnp.int32, (TOK, TOK), 1
    )
    before = earlier.astype(BF)
    rank0 = mm(hot0.astype(BF), before)
    rank1 = mm(hot1.astype(BF), before) + jnp.sum(hot0, axis=1, keepdims=True)
    pos0 = jnp.sum(hot0 * rank0, axis=0, keepdims=True).astype(jnp.int32)
    pos1 = jnp.sum(hot1 * rank1, axis=0, keepdims=True).astype(jnp.int32)
    return first * 16 + pos0, second * 16 + pos1


def row_hot(slot, half):
    row = lax.broadcasted_iota(jnp.int32, (ROWS, TOK), 0)
    return ((row >> 3) * 16 + half * 8 + (row & 7)) == slot


def hot_of(slots, half):
    return jnp.logical_or(row_hot(slots[0], half), row_hot(slots[1], half)).astype(BF)


def prob_of(slots, prob_ref, half):
    weight = jnp.zeros((ROWS, TOK), F32)
    for k in range(2):
        weight += jnp.where(row_hot(slots[k], half), prob_ref[k : k + 1, :].astype(F32), 0.0)
    return jnp.sum(weight, axis=1, keepdims=True)


def send_ring_kernel(
    z_ref, ids_hbm, prob_hbm, tok_hbm, grad_hbm, out_ref, ids_ref, prob_ref, buf, sems
):
    z = z_ref[0]
    c_ids = pltpu.make_async_copy(ids_hbm, ids_ref, sems.at[0])
    c_prob = pltpu.make_async_copy(prob_hbm, prob_ref, sems.at[1])
    c_ids.start()
    c_prob.start()
    cols = pl.ds(pl.multiple_of(lax.rem(z, 4) * QUARTER, 128), QUARTER)
    of_tokens = pltpu.make_async_copy(tok_hbm.at[:, cols], buf, sems.at[2])
    of_grads = pltpu.make_async_copy(grad_hbm.at[:, cols], buf, sems.at[2])

    @pl.when(z < 4)
    def _():
        of_tokens.start()

    @pl.when(z >= 4)
    def _():
        of_grads.start()

    c_ids.wait()
    slots = slots_of(ids_ref)
    hot = hot_of(slots, 0)
    c_prob.wait()
    prob = jnp.where(z < 4, 1.0, prob_of(slots, prob_ref, 0))
    of_tokens.wait()
    out_ref[...] = (mm(hot, buf[...]) * prob).astype(BF)


def send_plane_kernel(
    ids_hbm, prob_hbm, tok_hbm, grad_hbm, out_ref, ids_ref, prob_ref, tok_ref, grad_ref, sems
):
    copies = [
        pltpu.make_async_copy(src, dst, sems.at[i])
        for i, (src, dst) in enumerate(
            ((ids_hbm, ids_ref), (prob_hbm, prob_ref), (tok_hbm, tok_ref), (grad_hbm, grad_ref))
        )
    ]
    for c in copies:
        c.start()
    copies[0].wait()
    slots = slots_of(ids_ref)
    hot = hot_of(slots, 1)
    copies[1].wait()
    prob = prob_of(slots, prob_ref, 1)
    copies[2].wait()
    copies[3].wait()
    for c in range(0, D, QUARTER):
        out_ref[:, c : c + QUARTER] = mm(hot, tok_ref[:, c : c + QUARTER]).astype(BF)
        out_ref[:, D + c : D + c + QUARTER] = (
            mm(hot, grad_ref[:, c : c + QUARTER]) * prob
        ).astype(BF)


def quarter(q):
    return pl.ds(q * QUARTER, QUARTER)


def expert_kernel(offsets, z_ref, *refs):
    shards = refs[:16]
    both_hbm, down_hbm, gate_hbm, up_hbm = refs[16:20]
    packs = refs[20:36]
    score_ref, hid_ref, rows_hbm = refs[36:39]
    ring, plane, down_w, gate_w, up_w, gate_grad_ref, up_grad_ref, part = refs[39:47]
    values, stage, ring_sems, sems, out_sems = refs[47:]
    z = z_ref[0]
    c_x, c_rows = (
        pltpu.make_async_copy(both_hbm.at[:, i * D : (i + 1) * D], plane.at[i], sems.at[i])
        for i in range(2)
    )
    c_down, c_gate, c_up = (
        pltpu.make_async_copy(src, dst, sems.at[2 + i])
        for i, (src, dst) in enumerate(
            ((down_hbm, down_w), (gate_hbm, gate_w), (up_hbm, up_w))
        )
    )
    c_x.start()
    c_gate.start()
    by_ring = []
    for chain in range(2):
        here = pl.ds(chain * 128, 128)
        for i, off in enumerate(offsets[chain]):
            owner = lax.rem(z + off + 8, 8)
            cols = pl.ds(pl.multiple_of(lax.rem(owner, 4) * QUARTER, 128), QUARTER)
            by_ring.append(
                pltpu.make_async_copy(
                    shards[8 * chain + i], ring.at[owner // 4, here, cols], ring_sems.at[chain, i]
                )
            )

    def ahead(gate, up, back, base):
        sig = jax.nn.sigmoid(gate)
        hidden = (gate * sig * up).astype(BF)
        here = pl.ds(base, ROWS)
        hid_ref[here, :] = hidden
        up_grad_ref[here, :] = (back * gate * sig).astype(BF)
        gate_grad_ref[here, :] = (back * up * sig * (1.0 + gate * (1.0 - sig))).astype(BF)
        score = jnp.sum(back * hidden.astype(F32), axis=1, keepdims=True)
        score_ref[here, :] = jnp.broadcast_to(score, (ROWS, 128)).astype(BF)

    c_x.wait()
    c_gate.wait()
    c_up.start()
    values[0] = mm(plane[0], gate_w[...], NT)
    c_up.wait()
    c_rows.start()
    c_down.start()
    values[1] = mm(plane[0], up_w[...], NT)
    c_rows.wait()
    c_down.wait()
    for c in by_ring:
        c.start()
    values[2] = mm(plane[1], down_w[...], NT)
    ahead(values[0], values[1], values[2], ROWS)
    for c in by_ring:
        c.wait()
    rows_out = pltpu.make_async_copy(ring.at[1], rows_hbm, out_sems.at[16])
    rows_out.start()
    ahead(
        mm(ring[0], gate_w[...], NT),
        mm(ring[0], up_w[...], NT),
        mm(ring[1], down_w[...], NT),
        0,
    )
    for c in range(0, D, QUARTER):
        part[:, c : c + QUARTER] = (
            mm(gate_grad_ref[...], gate_w[:, c : c + QUARTER])
            + mm(up_grad_ref[...], up_w[:, c : c + QUARTER])
        ).astype(BF)
    lane = lax.broadcasted_iota(jnp.int32, (128, 128), 1)
    out_copies = []
    for r in (4, 5, 3, 6, 2, 7, 1, 0):
        shard = lax.rem(z + r, 8)
        cols = pl.ds(pl.multiple_of(shard * WIDE, 128), WIDE)
        tile = pl.ds(pl.multiple_of((24 + shard // 2) * 128, 128), 128)
        odd = lax.rem(shard, 2) == 1
        for half in range(2):
            i = 8 * half + r
            base = half * ROWS
            stage[i, :, :WIDE] = part[base : base + 128, cols]
            stage[i, :, WIDE : 2 * WIDE] = part[base + 128 : base + 256, cols]
            top = part[base : base + 128, tile].astype(F32)
            bottom = part[base + 128 : base + 256, tile].astype(F32)
            top = jnp.where(odd, pltpu.roll(top, 64, 1), top)
            bottom = jnp.where(odd, bottom, pltpu.roll(bottom, 64, 1))
            stage[i, :, 2 * WIDE :] = jnp.where(lane < 64, top, bottom).astype(BF)
            c = pltpu.make_async_copy(stage.at[i], packs[i], out_sems.at[i])
            c.start()
            out_copies.append(c)
    for c in out_copies:
        c.wait()
    rows_out.wait()


def back_kernel(*refs):
    out_ref = refs[7]
    lane = lax.broadcasted_iota(jnp.int32, (128, 128), 1)
    tiles = []
    for half in range(2):
        own, left, right = refs[3 * half : 3 * half + 3]
        total = (
            own[...].astype(F32) + left[...].astype(F32) + right[...].astype(F32)
        )
        base = half * WIDE
        out_ref[0:128, base : base + WIDE] = total[:, :WIDE].astype(BF)
        out_ref[128:256, base : base + WIDE] = total[:, WIDE : 2 * WIDE].astype(BF)
        tile = total[:, 2 * WIDE :]
        tiles.append((tile, pltpu.roll(tile, 64, 1)))
    (t0, r0), (t1, r1) = tiles
    out_ref[0:128, 2 * WIDE : PACK] = jnp.where(lane < 64, t0, r1).astype(BF)
    out_ref[128:256, 2 * WIDE : PACK] = jnp.where(lane < 64, r0, t1).astype(BF)
    score0, score1 = refs[6][0:ROWS, :], refs[6][ROWS:, :]
    wide = lax.broadcasted_iota(jnp.int32, (ROWS, 128), 1)
    out_ref[:, PACK:] = jnp.where(
        wide == 0, score0.astype(F32), jnp.where(wide == 1, score1.astype(F32), 0.0)
    ).astype(BF)


def token_sum_kernel(ids_ref, got_ref, out_ref):
    slot0, slot1 = slots_of(ids_ref)
    hots = [
        [row_hot(slot, half).astype(BF) for slot in (slot0, slot1)] for half in range(2)
    ]
    both = [h[0] + h[1] for h in hots]
    out_ref[:, :WIDE] = (
        mm(both[0], got_ref[:, :WIDE], TN) + mm(both[1], got_ref[:, WIDE : 2 * WIDE], TN)
    ).astype(BF)
    tile = got_ref[:, 2 * WIDE : PACK]
    low = mm(both[0], tile, TN)
    high = pltpu.roll(mm(both[1], tile, TN), 64, 1)
    scores = got_ref[:, PACK:]
    lane = lax.broadcasted_iota(jnp.int32, (128, 128), 1)
    result = jnp.where(lane < 64, low + high, 0.0)
    for k in range(2):
        total = mm(hots[0][k], scores, TN)[:, 0:1] + mm(hots[1][k], scores, TN)[:, 1:2]
        result = jnp.where(lane == 64 + k, total, result)
    out_ref[:, WIDE:] = result.astype(BF)


def assemble_kernel(offsets, z_ref, prob_in, *refs):
    shards = refs[:8]
    out_ref, prob_ref, tiles = refs[8:]
    z = z_ref[0]
    total = jnp.zeros((128, 128), F32)
    for i, off in enumerate(offsets):
        owner = lax.rem(z + off + 8, 8)
        cols = pl.ds(pl.multiple_of(owner * WIDE, 128), WIDE)
        out_ref[:, cols] = shards[i][:, :WIDE]
        tile = shards[i][:, WIDE:].astype(F32)
        tiles[owner] = tile
        total = total + tile
    prob_ref[...] = (total.T[64:66, :] / prob_in[...].astype(F32)).astype(BF)
    lane = lax.broadcasted_iota(jnp.int32, (128, 128), 1)
    for j in range(4):
        c = 8 * WIDE + 128 * j
        out_ref[:, c : c + 128] = jnp.where(
            lane < 64, tiles[2 * j], pltpu.roll(tiles[2 * j + 1], 64, 1)
        ).astype(BF)


def down_kernel(hid_ref, rows0, rows1, out_ref):
    out_ref[...] = (
        mm(hid_ref[0:ROWS, :], rows0[...], TN) + mm(hid_ref[ROWS:, :], rows1[...], TN)
    ).astype(BF)


OFFSETS = ((0, -1, 1, -2, 2, -3, 3, -4), (0, 1, -1, 2, -2, 3, -3, 4))


def hop(x, by):
    return lax.ppermute(x, "etp", [(i, (i + by) % N_Z) for i in range(N_Z)])


def ring_gather(x, way):
    shards = [x]
    far = near = x
    for step in range(4):
        far = hop(far, way)
        shards.append(far)
        if step < 3:
            near = hop(near, -way)
            shards.append(near)
    return shards


def add_rows(a, b):
    return (a.astype(F32) + b.astype(F32)).astype(BF)


def ring_scatter(packs, sums, way):
    far, near = sums
    for step in range(3):
        far = hop(add_rows(far, packs[4 - way * (step + 1)]), way)
        if step < 2:
            near = hop(add_rows(near, packs[4 + way * (step + 2)]), -way)
    return far, near


def exchange(x):
    return lax.all_to_all(x, "ep", split_axis=0, concat_axis=0, tiled=True)


def shape(*dims, dtype=BF):
    return jax.ShapeDtypeStruct(dims, dtype)


def on_device(tokens, out_grad, expert_ids, route_probs, w_gate, w_up, w_down):
    z = lax.axis_index("etp").astype(jnp.int32).reshape(1)
    ids = expert_ids.T
    probs = route_probs.T
    gate_w = w_gate[0].T
    up_w = w_up[0].T
    down_w = w_down[0]

    small = [
        pltpu.VMEM((2, TOK), jnp.int32),
        pltpu.VMEM((2, TOK), BF),
    ]
    send_ring = pl.pallas_call(
        send_ring_kernel,
        out_shape=shape(ROWS, QUARTER),
        in_specs=[SM] + [HBM] * 4,
        out_specs=VM,
        scratch_shapes=small + [pltpu.VMEM((TOK, QUARTER), BF), pltpu.SemaphoreType.DMA((3,))],
        compiler_params=params(60),
        name="send_ring",
    )(z, ids, probs, tokens, out_grad)
    got_ring = exchange(send_ring.reshape(EXPERTS, 8, QUARTER)).reshape(ROWS, QUARTER)
    send_plane = pl.pallas_call(
        send_plane_kernel,
        out_shape=shape(ROWS, 2 * D),
        in_specs=[HBM] * 4,
        out_specs=VM,
        scratch_shapes=small
        + [pltpu.VMEM((TOK, D), BF)] * 2
        + [pltpu.SemaphoreType.DMA((4,))],
        compiler_params=params(60),
        name="send_plane",
    )(ids, probs, tokens, out_grad)
    got_plane = exchange(send_plane.reshape(EXPERTS, 8, 2 * D)).reshape(ROWS, 2 * D)
    chains = ring_gather(got_ring[:128], 1) + ring_gather(got_ring[128:], -1)

    *packs, score, hidden, ring_rows = pl.pallas_call(
        functools.partial(expert_kernel, OFFSETS),
        out_shape=[shape(128, PACK)] * 16
        + [shape(2 * ROWS, 128), shape(2 * ROWS, UNITS), shape(ROWS, D)],
        in_specs=[SM] + [HBM] * 20,
        out_specs=[HBM] * 16 + [VM] * 2 + [HBM],
        scratch_shapes=[pltpu.VMEM((2, ROWS, D), BF)] * 2
        + [pltpu.VMEM((UNITS, D), BF)] * 3
        + [pltpu.VMEM((2 * ROWS, UNITS), BF)] * 2
        + [
            pltpu.VMEM((2 * ROWS, D), BF),
            pltpu.VMEM((3, ROWS, UNITS), F32),
            pltpu.VMEM((16, 128, PACK), BF),
            pltpu.SemaphoreType.DMA((2, 8)),
            pltpu.SemaphoreType.DMA((5,)),
            pltpu.SemaphoreType.DMA((17,)),
        ],
        compiler_params=params(60),
        name="expert",
    )(z, *chains, got_plane, down_w, gate_w, up_w)
    packs0, packs1 = packs[:8], packs[8:]
    sums0 = (hop(packs0[4], 1), hop(packs0[5], -1))
    sums1 = (hop(packs1[4], -1), hop(packs1[3], 1))
    back_parts = [
        packs0[0],
        *ring_scatter(packs0, sums0, 1),
        packs1[0],
        *ring_scatter(packs1, sums1, -1),
        score,
    ]

    send_back = pl.pallas_call(
        back_kernel,
        out_shape=shape(ROWS, PACK + 128),
        in_specs=[VM] * 7,
        out_specs=VM,
        compiler_params=params(),
        name="pack_back",
    )(*back_parts)
    got_back = exchange(send_back.reshape(EXPERTS, 8, PACK + 128)).reshape(ROWS, PACK + 128)
    summed = pl.pallas_call(
        token_sum_kernel,
        out_shape=shape(TOK, 512),
        in_specs=[VM] * 2,
        out_specs=VM,
        compiler_params=params(),
        name="token_sum",
    )(ids, got_back)
    token_grad, prob_grad = pl.pallas_call(
        functools.partial(assemble_kernel, OFFSETS[0]),
        out_shape=[shape(TOK, D), shape(2, TOK)],
        in_specs=[SM] + [VM] * 9,
        out_specs=[VM] * 2,
        scratch_shapes=[pltpu.VMEM((8, 128, 128), F32)],
        compiler_params=params(),
        name="assemble",
    )(z, probs, *ring_gather(summed, 1))

    down_grad = pl.pallas_call(
        down_kernel,
        out_shape=shape(UNITS, D),
        grid=(4,),
        in_specs=[
            pl.BlockSpec((2 * ROWS, UNITS), lambda i: (0, 0)),
            pl.BlockSpec((ROWS, QUARTER), lambda i: (0, i)),
            pl.BlockSpec((ROWS, QUARTER), lambda i: (0, 4 + i)),
        ],
        out_specs=pl.BlockSpec((UNITS, QUARTER), lambda i: (0, i)),
        compiler_params=params(),
        name="down_grad",
    )(hidden, ring_rows, got_plane)
    return (token_grad, prob_grad.T, down_grad[None])


def solution(mesh):
    return jax.shard_map(
        on_device,
        mesh=mesh,
        in_specs=(
            P("ep", None),
            P("ep", None),
            P("ep", None),
            P("ep", None),
            P("ep", None, "etp"),
            P("ep", None, "etp"),
            P("ep", "etp", None),
        ),
        out_specs=(P("ep", None), P("ep", None), P("ep", "etp", None)),
        check_vma=False,
    )
```

```python
import functools

import jax
import jax.numpy as jnp
from jax import lax
from jax.experimental import pallas as pl
from jax.experimental.pallas import tpu as pltpu
from jax.sharding import PartitionSpec as P

D = 3584
UNITS = 400
TOK = 128
EXPERTS = 32
N_Z = 8
ROWS = 256
QUARTER = D // 4
WIDE = 384
PACK = 2 * WIDE + 128
BF = jnp.bfloat16
F32 = jnp.float32

NT = (((1,), (1,)), ((), ()))
TN = (((0,), (0,)), ((), ()))
NN = (((1,), (0,)), ((), ()))


def mm(left, right, dims=NN):
    return lax.dot_general(left, right, dims, preferred_element_type=F32)


def params(mib=20):
    return pltpu.CompilerParams(vmem_limit_bytes=mib * 2**20)


VM = pl.BlockSpec(memory_space=pltpu.VMEM)
SM = pl.BlockSpec(memory_space=pltpu.SMEM)
HBM = pl.BlockSpec(memory_space=pltpu.HBM)


def slots_of(ids_ref):
    expert = lax.broadcasted_iota(jnp.int32, (EXPERTS, TOK), 0)
    first = ids_ref[0:1, :]
    second = ids_ref[1:2, :]
    hot0 = (expert == first).astype(F32)
    hot1 = (expert == second).astype(F32)
    earlier = lax.broadcasted_iota(jnp.int32, (TOK, TOK), 0) < lax.broadcasted_iota(
        jnp.int32, (TOK, TOK), 1
    )
    before = earlier.astype(BF)
    rank0 = mm(hot0.astype(BF), before)
    rank1 = mm(hot1.astype(BF), before) + jnp.sum(hot0, axis=1, keepdims=True)
    pos0 = jnp.sum(hot0 * rank0, axis=0, keepdims=True).astype(jnp.int32)
    pos1 = jnp.sum(hot1 * rank1, axis=0, keepdims=True).astype(jnp.int32)
    return first * 16 + pos0, second * 16 + pos1


def row_hot(slot, half):
    row = lax.broadcasted_iota(jnp.int32, (ROWS, TOK), 0)
    return ((row >> 3) * 16 + half * 8 + (row & 7)) == slot


def hot_of(slots, half):
    return jnp.logical_or(row_hot(slots[0], half), row_hot(slots[1], half)).astype(BF)


def prob_of(slots, prob_ref, half):
    weight = jnp.zeros((ROWS, TOK), F32)
    for k in range(2):
        weight += jnp.where(row_hot(slots[k], half), prob_ref[k : k + 1, :].astype(F32), 0.0)
    return jnp.sum(weight, axis=1, keepdims=True)


def send_ring_kernel(
    z_ref, ids_hbm, prob_hbm, tok_hbm, grad_hbm, out_ref, ids_ref, prob_ref, buf, sems
):
    z = z_ref[0]
    c_ids = pltpu.make_async_copy(ids_hbm, ids_ref, sems.at[0])
    c_prob = pltpu.make_async_copy(prob_hbm, prob_ref, sems.at[1])
    c_ids.start()
    c_prob.start()
    cols = pl.ds(pl.multiple_of(lax.rem(z, 4) * QUARTER, 128), QUARTER)
    of_tokens = pltpu.make_async_copy(tok_hbm.at[:, cols], buf, sems.at[2])
    of_grads = pltpu.make_async_copy(grad_hbm.at[:, cols], buf, sems.at[2])

    @pl.when(z < 4)
    def _():
        of_tokens.start()

    @pl.when(z >= 4)
    def _():
        of_grads.start()

    c_ids.wait()
    slots = slots_of(ids_ref)
    hot = hot_of(slots, 0)
    c_prob.wait()
    prob = jnp.where(z < 4, 1.0, prob_of(slots, prob_ref, 0))
    of_tokens.wait()
    out_ref[...] = (mm(hot, buf[...]) * prob).astype(BF)


def send_plane_kernel(
    ids_hbm, prob_hbm, tok_hbm, grad_hbm, out_ref, ids_ref, prob_ref, tok_ref, grad_ref, sems
):
    copies = [
        pltpu.make_async_copy(src, dst, sems.at[i])
        for i, (src, dst) in enumerate(
            ((ids_hbm, ids_ref), (prob_hbm, prob_ref), (tok_hbm, tok_ref), (grad_hbm, grad_ref))
        )
    ]
    for c in copies:
        c.start()
    copies[0].wait()
    slots = slots_of(ids_ref)
    hot = hot_of(slots, 1)
    copies[1].wait()
    prob = prob_of(slots, prob_ref, 1)
    copies[2].wait()
    copies[3].wait()
    for c in range(0, D, QUARTER):
        out_ref[:, c : c + QUARTER] = mm(hot, tok_ref[:, c : c + QUARTER]).astype(BF)
        out_ref[:, D + c : D + c + QUARTER] = (
            mm(hot, grad_ref[:, c : c + QUARTER]) * prob
        ).astype(BF)


def quarter(q):
    return pl.ds(q * QUARTER, QUARTER)


def expert_kernel(offsets, z_ref, *refs):
    shards = refs[:16]
    both_hbm, down_hbm, gate_hbm, up_hbm = refs[16:20]
    packs = refs[20:36]
    score_ref, hid_ref, rows_hbm = refs[36:39]
    ring, plane, down_w, gate_w, up_w, gate_grad_ref, up_grad_ref, part = refs[39:47]
    values, stage, ring_sems, sems, out_sems = refs[47:]
    z = z_ref[0]
    c_x, c_rows = (
        pltpu.make_async_copy(both_hbm.at[:, i * D : (i + 1) * D], plane.at[i], sems.at[i])
        for i in range(2)
    )
    c_down, c_gate, c_up = (
        pltpu.make_async_copy(src, dst, sems.at[2 + i])
        for i, (src, dst) in enumerate(
            ((down_hbm, down_w), (gate_hbm, gate_w), (up_hbm, up_w))
        )
    )
    c_x.start()
    c_gate.start()
    by_ring = []
    for chain in range(2):
        here = pl.ds(chain * 128, 128)
        for i, off in enumerate(offsets[chain]):
            owner = lax.rem(z + off + 8, 8)
            cols = pl.ds(pl.multiple_of(lax.rem(owner, 4) * QUARTER, 128), QUARTER)
            by_ring.append(
                pltpu.make_async_copy(
                    shards[8 * chain + i], ring.at[owner // 4, here, cols], ring_sems.at[chain, i]
                )
            )

    def ahead(gate, up, back, base):
        sig = jax.nn.sigmoid(gate)
        hidden = (gate * sig * up).astype(BF)
        here = pl.ds(base, ROWS)
        hid_ref[here, :] = hidden
        up_grad_ref[here, :] = (back * gate * sig).astype(BF)
        gate_grad_ref[here, :] = (back * up * sig * (1.0 + gate * (1.0 - sig))).astype(BF)
        score = jnp.sum(back * hidden.astype(F32), axis=1, keepdims=True)
        score_ref[here, :] = jnp.broadcast_to(score, (ROWS, 128)).astype(BF)

    c_x.wait()
    c_gate.wait()
    c_up.start()
    values[0] = mm(plane[0], gate_w[...], NT)
    c_up.wait()
    c_rows.start()
    c_down.start()
    values[1] = mm(plane[0], up_w[...], NT)
    c_rows.wait()
    c_down.wait()
    for c in by_ring:
        c.start()
    values[2] = mm(plane[1], down_w[...], NT)
    ahead(values[0], values[1], values[2], ROWS)
    for c in by_ring:
        c.wait()
    rows_out = pltpu.make_async_copy(ring.at[1], rows_hbm, out_sems.at[16])
    rows_out.start()
    ahead(
        mm(ring[0], gate_w[...], NT),
        mm(ring[0], up_w[...], NT),
        mm(ring[1], down_w[...], NT),
        0,
    )
    for c in range(0, D, QUARTER):
        part[:, c : c + QUARTER] = (
            mm(gate_grad_ref[...], gate_w[:, c : c + QUARTER])
            + mm(up_grad_ref[...], up_w[:, c : c + QUARTER])
        ).astype(BF)
    lane = lax.broadcasted_iota(jnp.int32, (128, 128), 1)
    out_copies = []
    for r in (4, 5, 3, 6, 2, 7, 1, 0):
        shard = lax.rem(z + r, 8)
        cols = pl.ds(pl.multiple_of(shard * WIDE, 128), WIDE)
        tile = pl.ds(pl.multiple_of((24 + shard // 2) * 128, 128), 128)
        odd = lax.rem(shard, 2) == 1
        for half in range(2):
            i = 8 * half + r
            base = half * ROWS
            stage[i, :, :WIDE] = part[base : base + 128, cols]
            stage[i, :, WIDE : 2 * WIDE] = part[base + 128 : base + 256, cols]
            top = part[base : base + 128, tile].astype(F32)
            bottom = part[base + 128 : base + 256, tile].astype(F32)
            top = jnp.where(odd, pltpu.roll(top, 64, 1), top)
            bottom = jnp.where(odd, bottom, pltpu.roll(bottom, 64, 1))
            stage[i, :, 2 * WIDE :] = jnp.where(lane < 64, top, bottom).astype(BF)
            c = pltpu.make_async_copy(stage.at[i], packs[i], out_sems.at[i])
            c.start()
            out_copies.append(c)
    for c in out_copies:
        c.wait()
    rows_out.wait()


def back_kernel(*refs):
    out_ref = refs[7]
    lane = lax.broadcasted_iota(jnp.int32, (128, 128), 1)
    tiles = []
    for half in range(2):
        own, left, right = refs[3 * half : 3 * half + 3]
        total = (
            own[...].astype(F32) + left[...].astype(F32) + right[...].astype(F32)
        )
        base = half * WIDE
        out_ref[0:128, base : base + WIDE] = total[:, :WIDE].astype(BF)
        out_ref[128:256, base : base + WIDE] = total[:, WIDE : 2 * WIDE].astype(BF)
        tile = total[:, 2 * WIDE :]
        tiles.append((tile, pltpu.roll(tile, 64, 1)))
    (t0, r0), (t1, r1) = tiles
    out_ref[0:128, 2 * WIDE : PACK] = jnp.where(lane < 64, t0, r1).astype(BF)
    out_ref[128:256, 2 * WIDE : PACK] = jnp.where(lane < 64, r0, t1).astype(BF)
    score0, score1 = refs[6][0:ROWS, :], refs[6][ROWS:, :]
    wide = lax.broadcasted_iota(jnp.int32, (ROWS, 128), 1)
    out_ref[:, PACK:] = jnp.where(
        wide == 0, score0.astype(F32), jnp.where(wide == 1, score1.astype(F32), 0.0)
    ).astype(BF)


def token_sum_kernel(ids_ref, got_ref, out_ref):
    slot0, slot1 = slots_of(ids_ref)
    hots = [
        [row_hot(slot, half).astype(BF) for slot in (slot0, slot1)] for half in range(2)
    ]
    both = [h[0] + h[1] for h in hots]
    wide = mm(both[0], got_ref[:, :WIDE], TN) + mm(both[1], got_ref[:, WIDE : 2 * WIDE], TN)
    for k in range(3):
        out_ref[128 * k : 128 * k + 128, :] = wide[:, 128 * k : 128 * k + 128].astype(BF)
    tile = got_ref[:, 2 * WIDE : PACK]
    half_tile = mm(both[0], tile, TN) + pltpu.roll(mm(both[1], tile, TN), 64, 1)
    lane = lax.broadcasted_iota(jnp.int32, (64, 128), 1)
    out_ref[WIDE : WIDE + 64, :] = jnp.where(
        lane < 64, half_tile[:64], pltpu.roll(half_tile[64:], 64, 1)
    ).astype(BF)
    scores = got_ref[:, PACK:]
    row = lax.broadcasted_iota(jnp.int32, (16, 128), 0)
    result = jnp.zeros((16, 128), F32)
    for k in range(2):
        total = mm(scores, hots[0][k], TN)[0:1, :] + mm(scores, hots[1][k], TN)[1:2, :]
        result = jnp.where(row == k, total, result)
    out_ref[WIDE + 64 :, :] = result.astype(BF)


def assemble_kernel(prob_in, all_ref, out_ref, prob_ref):
    for i in range(8):
        for k in range(3):
            c = WIDE * i + 128 * k
            out_ref[:, c : c + 128] = all_ref[i, 128 * k : 128 * k + 128, :]
    lane = lax.broadcasted_iota(jnp.int32, (64, 128), 1)
    for j in range(4):
        c = 8 * WIDE + 128 * j
        even = all_ref[2 * j, WIDE : WIDE + 64, :].astype(F32)
        odd = all_ref[2 * j + 1, WIDE : WIDE + 64, :].astype(F32)
        out_ref[0:64, c : c + 128] = jnp.where(lane < 64, even, pltpu.roll(odd, 64, 1)).astype(BF)
        out_ref[64:128, c : c + 128] = jnp.where(lane < 64, pltpu.roll(even, 64, 1), odd).astype(BF)
    total = all_ref[0, WIDE + 64 :, :].astype(F32)
    for i in range(1, 8):
        total = total + all_ref[i, WIDE + 64 :, :].astype(F32)
    prob_ref[...] = (total[0:2, :] / prob_in[...].astype(F32)).astype(BF)


def down_kernel(hid_ref, rows0, rows1, out_ref):
    out_ref[...] = (
        mm(hid_ref[0:ROWS, :], rows0[...], TN) + mm(hid_ref[ROWS:, :], rows1[...], TN)
    ).astype(BF)


OFFSETS = ((0, -1, 1, -2, 2, -3, 3, -4), (0, 1, -1, 2, -2, 3, -3, 4))


def hop(x, by):
    return lax.ppermute(x, "etp", [(i, (i + by) % N_Z) for i in range(N_Z)])


def ring_gather(x, way):
    shards = [x]
    far = near = x
    for step in range(4):
        far = hop(far, way)
        shards.append(far)
        if step < 3:
            near = hop(near, -way)
            shards.append(near)
    return shards


def add_rows(a, b):
    return (a.astype(F32) + b.astype(F32)).astype(BF)


def ring_scatter(packs, sums, way):
    far, near = sums
    for step in range(3):
        far = hop(add_rows(far, packs[4 - way * (step + 1)]), way)
        if step < 2:
            near = hop(add_rows(near, packs[4 + way * (step + 2)]), -way)
    return far, near


def exchange(x):
    return lax.all_to_all(x, "ep", split_axis=0, concat_axis=0, tiled=True)


def shape(*dims, dtype=BF):
    return jax.ShapeDtypeStruct(dims, dtype)


def on_device(tokens, out_grad, expert_ids, route_probs, w_gate, w_up, w_down):
    z = lax.axis_index("etp").astype(jnp.int32).reshape(1)
    ids = expert_ids.T
    probs = route_probs.T
    gate_w = w_gate[0].T
    up_w = w_up[0].T
    down_w = w_down[0]

    small = [
        pltpu.VMEM((2, TOK), jnp.int32),
        pltpu.VMEM((2, TOK), BF),
    ]
    send_ring = pl.pallas_call(
        send_ring_kernel,
        out_shape=shape(ROWS, QUARTER),
        in_specs=[SM] + [HBM] * 4,
        out_specs=VM,
        scratch_shapes=small + [pltpu.VMEM((TOK, QUARTER), BF), pltpu.SemaphoreType.DMA((3,))],
        compiler_params=params(60),
        name="send_ring",
    )(z, ids, probs, tokens, out_grad)
    got_ring = exchange(send_ring.reshape(EXPERTS, 8, QUARTER)).reshape(ROWS, QUARTER)
    send_plane = pl.pallas_call(
        send_plane_kernel,
        out_shape=shape(ROWS, 2 * D),
        in_specs=[HBM] * 4,
        out_specs=VM,
        scratch_shapes=small
        + [pltpu.VMEM((TOK, D), BF)] * 2
        + [pltpu.SemaphoreType.DMA((4,))],
        compiler_params=params(60),
        name="send_plane",
    )(ids, probs, tokens, out_grad)
    got_plane = exchange(send_plane.reshape(EXPERTS, 8, 2 * D)).reshape(ROWS, 2 * D)
    chains = ring_gather(got_ring[:128], 1) + ring_gather(got_ring[128:], -1)

    *packs, score, hidden, ring_rows = pl.pallas_call(
        functools.partial(expert_kernel, OFFSETS),
        out_shape=[shape(128, PACK)] * 16
        + [shape(2 * ROWS, 128), shape(2 * ROWS, UNITS), shape(ROWS, D)],
        in_specs=[SM] + [HBM] * 20,
        out_specs=[HBM] * 16 + [VM] * 2 + [HBM],
        scratch_shapes=[pltpu.VMEM((2, ROWS, D), BF)] * 2
        + [pltpu.VMEM((UNITS, D), BF)] * 3
        + [pltpu.VMEM((2 * ROWS, UNITS), BF)] * 2
        + [
            pltpu.VMEM((2 * ROWS, D), BF),
            pltpu.VMEM((3, ROWS, UNITS), F32),
            pltpu.VMEM((16, 128, PACK), BF),
            pltpu.SemaphoreType.DMA((2, 8)),
            pltpu.SemaphoreType.DMA((5,)),
            pltpu.SemaphoreType.DMA((17,)),
        ],
        compiler_params=params(60),
        name="expert",
    )(z, *chains, got_plane, down_w, gate_w, up_w)
    packs0, packs1 = packs[:8], packs[8:]
    sums0 = (hop(packs0[4], 1), hop(packs0[5], -1))
    sums1 = (hop(packs1[4], -1), hop(packs1[3], 1))
    back_parts = [
        packs0[0],
        *ring_scatter(packs0, sums0, 1),
        packs1[0],
        *ring_scatter(packs1, sums1, -1),
        score,
    ]

    send_back = pl.pallas_call(
        back_kernel,
        out_shape=shape(ROWS, PACK + 128),
        in_specs=[VM] * 7,
        out_specs=VM,
        compiler_params=params(),
        name="pack_back",
    )(*back_parts)
    got_back = exchange(send_back.reshape(EXPERTS, 8, PACK + 128)).reshape(ROWS, PACK + 128)
    down_grad = pl.pallas_call(
        down_kernel,
        out_shape=shape(UNITS, D),
        grid=(4,),
        in_specs=[
            pl.BlockSpec((2 * ROWS, UNITS), lambda i: (0, 0)),
            pl.BlockSpec((ROWS, QUARTER), lambda i: (0, i)),
            pl.BlockSpec((ROWS, QUARTER), lambda i: (0, 4 + i)),
        ],
        out_specs=pl.BlockSpec((UNITS, QUARTER), lambda i: (0, i)),
        compiler_params=params(),
        name="down_grad",
    )(hidden, ring_rows, got_plane)
    got_back, down_grad = lax.optimization_barrier((got_back, down_grad))
    summed = pl.pallas_call(
        token_sum_kernel,
        out_shape=shape(464, 128),
        in_specs=[VM] * 2,
        out_specs=VM,
        compiler_params=params(),
        name="token_sum",
    )(ids, got_back)
    token_grad, prob_grad = pl.pallas_call(
        assemble_kernel,
        out_shape=[shape(TOK, D), shape(2, TOK)],
        in_specs=[VM] * 2,
        out_specs=[VM] * 2,
        compiler_params=params(),
        name="assemble",
    )(probs, lax.all_gather(summed, "etp", axis=0, tiled=False))
    return (token_grad, prob_grad.T, down_grad[None])


def solution(mesh):
    return jax.shard_map(
        on_device,
        mesh=mesh,
        in_specs=(
            P("ep", None),
            P("ep", None),
            P("ep", None),
            P("ep", None),
            P("ep", None, "etp"),
            P("ep", None, "etp"),
            P("ep", "etp", None),
        ),
        out_specs=(P("ep", None), P("ep", None), P("ep", "etp", None)),
        check_vma=False,
    )
```

```python
import functools

import jax
import jax.numpy as jnp
from jax import lax
from jax.experimental import pallas as pl
from jax.experimental.pallas import tpu as pltpu
from jax.sharding import PartitionSpec as P

D = 3584
UNITS = 400
TOK = 128
EXPERTS = 32
N_Z = 8
ROWS = 256
QUARTER = D // 4
WIDE = 384
PACK = 2 * WIDE + 128
BF = jnp.bfloat16
F32 = jnp.float32

NT = (((1,), (1,)), ((), ()))
TN = (((0,), (0,)), ((), ()))
NN = (((1,), (0,)), ((), ()))


def mm(left, right, dims=NN):
    return lax.dot_general(left, right, dims, preferred_element_type=F32)


def params(mib=20):
    return pltpu.CompilerParams(vmem_limit_bytes=mib * 2**20)


VM = pl.BlockSpec(memory_space=pltpu.VMEM)
SM = pl.BlockSpec(memory_space=pltpu.SMEM)
HBM = pl.BlockSpec(memory_space=pltpu.HBM)


def slots_of(ids_ref):
    expert = lax.broadcasted_iota(jnp.int32, (EXPERTS, TOK), 0)
    first = ids_ref[0:1, :]
    second = ids_ref[1:2, :]
    hot0 = (expert == first).astype(F32)
    hot1 = (expert == second).astype(F32)
    earlier = lax.broadcasted_iota(jnp.int32, (TOK, TOK), 0) < lax.broadcasted_iota(
        jnp.int32, (TOK, TOK), 1
    )
    before = earlier.astype(BF)
    rank0 = mm(hot0.astype(BF), before)
    rank1 = mm(hot1.astype(BF), before) + jnp.sum(hot0, axis=1, keepdims=True)
    pos0 = jnp.sum(hot0 * rank0, axis=0, keepdims=True).astype(jnp.int32)
    pos1 = jnp.sum(hot1 * rank1, axis=0, keepdims=True).astype(jnp.int32)
    return first * 16 + pos0, second * 16 + pos1


def row_hot(slot, half):
    row = lax.broadcasted_iota(jnp.int32, (ROWS, TOK), 0)
    return ((row >> 3) * 16 + half * 8 + (row & 7)) == slot


def hot_of(slots, half):
    return jnp.logical_or(row_hot(slots[0], half), row_hot(slots[1], half)).astype(BF)


def prob_of(slots, prob_ref, half):
    weight = jnp.zeros((ROWS, TOK), F32)
    for k in range(2):
        weight += jnp.where(row_hot(slots[k], half), prob_ref[k : k + 1, :].astype(F32), 0.0)
    return jnp.sum(weight, axis=1, keepdims=True)


def send_ring_kernel(
    z_ref, ids_hbm, prob_hbm, tok_hbm, grad_hbm, out_ref, ids_ref, prob_ref, buf, sems
):
    z = z_ref[0]
    c_ids = pltpu.make_async_copy(ids_hbm, ids_ref, sems.at[0])
    c_prob = pltpu.make_async_copy(prob_hbm, prob_ref, sems.at[1])
    c_ids.start()
    c_prob.start()
    cols = pl.ds(pl.multiple_of(lax.rem(z, 4) * QUARTER, 128), QUARTER)
    of_tokens = pltpu.make_async_copy(tok_hbm.at[:, cols], buf, sems.at[2])
    of_grads = pltpu.make_async_copy(grad_hbm.at[:, cols], buf, sems.at[2])

    @pl.when(z < 4)
    def _():
        of_tokens.start()

    @pl.when(z >= 4)
    def _():
        of_grads.start()

    c_ids.wait()
    slots = slots_of(ids_ref)
    hot = hot_of(slots, 0)
    c_prob.wait()
    prob = jnp.where(z < 4, 1.0, prob_of(slots, prob_ref, 0))
    of_tokens.wait()
    out_ref[...] = (mm(hot, buf[...]) * prob).astype(BF)


def send_plane_kernel(
    ids_hbm, prob_hbm, tok_hbm, grad_hbm, out_ref, ids_ref, prob_ref, tok_ref, grad_ref, sems
):
    copies = [
        pltpu.make_async_copy(src, dst, sems.at[i])
        for i, (src, dst) in enumerate(
            ((ids_hbm, ids_ref), (prob_hbm, prob_ref), (tok_hbm, tok_ref), (grad_hbm, grad_ref))
        )
    ]
    for c in copies:
        c.start()
    copies[0].wait()
    slots = slots_of(ids_ref)
    hot = hot_of(slots, 1)
    copies[1].wait()
    prob = prob_of(slots, prob_ref, 1)
    copies[2].wait()
    copies[3].wait()
    for c in range(0, D, QUARTER):
        out_ref[:, c : c + QUARTER] = mm(hot, tok_ref[:, c : c + QUARTER]).astype(BF)
        out_ref[:, D + c : D + c + QUARTER] = (
            mm(hot, grad_ref[:, c : c + QUARTER]) * prob
        ).astype(BF)


def quarter(q):
    return pl.ds(q * QUARTER, QUARTER)


def expert_kernel(offsets, z_ref, *refs):
    shards = refs[:16]
    both_hbm, down_hbm, gate_hbm, up_hbm = refs[16:20]
    packs = refs[20:36]
    score_ref, hid_ref, rows_hbm = refs[36:39]
    ring, plane, down_w, gate_w, up_w, gate_grad_ref, up_grad_ref, part = refs[39:47]
    values, stage, ring_sems, sems, out_sems = refs[47:]
    z = z_ref[0]
    c_x, c_rows = (
        pltpu.make_async_copy(both_hbm.at[:, i * D : (i + 1) * D], plane.at[i], sems.at[i])
        for i in range(2)
    )
    c_down, c_gate, c_up = (
        pltpu.make_async_copy(src, dst, sems.at[2 + i])
        for i, (src, dst) in enumerate(
            ((down_hbm, down_w), (gate_hbm, gate_w), (up_hbm, up_w))
        )
    )
    for c in (c_x, c_gate, c_up, c_rows, c_down):
        c.start()
    by_ring = []
    for chain in range(2):
        here = pl.ds(chain * 128, 128)
        for i, off in enumerate(offsets[chain]):
            owner = lax.rem(z + off + 8, 8)
            cols = pl.ds(pl.multiple_of(lax.rem(owner, 4) * QUARTER, 128), QUARTER)
            by_ring.append(
                pltpu.make_async_copy(
                    shards[8 * chain + i], ring.at[owner // 4, here, cols], ring_sems.at[chain, i]
                )
            )

    def ahead(gate, up, back, base):
        sig = jax.nn.sigmoid(gate)
        hidden = (gate * sig * up).astype(BF)
        here = pl.ds(base, ROWS)
        hid_ref[here, :] = hidden
        up_grad_ref[here, :] = (back * gate * sig).astype(BF)
        gate_grad_ref[here, :] = (back * up * sig * (1.0 + gate * (1.0 - sig))).astype(BF)
        score = jnp.sum(back * hidden.astype(F32), axis=1, keepdims=True)
        score_ref[here, :] = jnp.broadcast_to(score, (ROWS, 128)).astype(BF)

    c_x.wait()
    c_gate.wait()
    for c in by_ring:
        c.start()
    values[0] = mm(plane[0], gate_w[...], NT)
    c_up.wait()
    values[1] = mm(plane[0], up_w[...], NT)
    c_rows.wait()
    c_down.wait()
    values[2] = mm(plane[1], down_w[...], NT)
    ahead(values[0], values[1], values[2], ROWS)
    for c in by_ring:
        c.wait()
    rows_out = pltpu.make_async_copy(ring.at[1], rows_hbm, out_sems.at[16])
    rows_out.start()
    ahead(
        mm(ring[0], gate_w[...], NT),
        mm(ring[0], up_w[...], NT),
        mm(ring[1], down_w[...], NT),
        0,
    )
    for c in range(0, D, QUARTER):
        part[:, c : c + QUARTER] = (
            mm(gate_grad_ref[...], gate_w[:, c : c + QUARTER])
            + mm(up_grad_ref[...], up_w[:, c : c + QUARTER])
        ).astype(BF)
    lane = lax.broadcasted_iota(jnp.int32, (128, 128), 1)
    out_copies = []
    for r in (4, 5, 3, 6, 2, 7, 1, 0):
        shard = lax.rem(z + r, 8)
        cols = pl.ds(pl.multiple_of(shard * WIDE, 128), WIDE)
        tile = pl.ds(pl.multiple_of((24 + shard // 2) * 128, 128), 128)
        odd = lax.rem(shard, 2) == 1
        for half in range(2):
            i = 8 * half + r
            base = half * ROWS
            stage[i, :, :WIDE] = part[base : base + 128, cols]
            stage[i, :, WIDE : 2 * WIDE] = part[base + 128 : base + 256, cols]
            top = part[base : base + 128, tile].astype(F32)
            bottom = part[base + 128 : base + 256, tile].astype(F32)
            top = jnp.where(odd, pltpu.roll(top, 64, 1), top)
            bottom = jnp.where(odd, bottom, pltpu.roll(bottom, 64, 1))
            stage[i, :, 2 * WIDE :] = jnp.where(lane < 64, top, bottom).astype(BF)
            c = pltpu.make_async_copy(stage.at[i], packs[i], out_sems.at[i])
            c.start()
            out_copies.append(c)
    for c in out_copies:
        c.wait()
    rows_out.wait()


def back_kernel(*refs):
    out_ref = refs[7]
    lane = lax.broadcasted_iota(jnp.int32, (128, 128), 1)
    tiles = []
    for half in range(2):
        own, left, right = refs[3 * half : 3 * half + 3]
        total = (
            own[...].astype(F32) + left[...].astype(F32) + right[...].astype(F32)
        )
        base = half * WIDE
        out_ref[0:128, base : base + WIDE] = total[:, :WIDE].astype(BF)
        out_ref[128:256, base : base + WIDE] = total[:, WIDE : 2 * WIDE].astype(BF)
        tile = total[:, 2 * WIDE :]
        tiles.append((tile, pltpu.roll(tile, 64, 1)))
    (t0, r0), (t1, r1) = tiles
    out_ref[0:128, 2 * WIDE : PACK] = jnp.where(lane < 64, t0, r1).astype(BF)
    out_ref[128:256, 2 * WIDE : PACK] = jnp.where(lane < 64, r0, t1).astype(BF)
    score0, score1 = refs[6][0:ROWS, :], refs[6][ROWS:, :]
    wide = lax.broadcasted_iota(jnp.int32, (ROWS, 128), 1)
    out_ref[:, PACK:] = jnp.where(
        wide == 0, score0.astype(F32), jnp.where(wide == 1, score1.astype(F32), 0.0)
    ).astype(BF)


def token_sum_kernel(ids_ref, got_ref, out_ref):
    slot0, slot1 = slots_of(ids_ref)
    hots = [
        [row_hot(slot, half).astype(BF) for slot in (slot0, slot1)] for half in range(2)
    ]
    both = [h[0] + h[1] for h in hots]
    wide = mm(both[0], got_ref[:, :WIDE], TN) + mm(both[1], got_ref[:, WIDE : 2 * WIDE], TN)
    for k in range(3):
        out_ref[128 * k : 128 * k + 128, :] = wide[:, 128 * k : 128 * k + 128].astype(BF)
    tile = got_ref[:, 2 * WIDE : PACK]
    half_tile = mm(both[0], tile, TN) + pltpu.roll(mm(both[1], tile, TN), 64, 1)
    lane = lax.broadcasted_iota(jnp.int32, (64, 128), 1)
    out_ref[WIDE : WIDE + 64, :] = jnp.where(
        lane < 64, half_tile[:64], pltpu.roll(half_tile[64:], 64, 1)
    ).astype(BF)
    scores = got_ref[:, PACK:]
    row = lax.broadcasted_iota(jnp.int32, (16, 128), 0)
    result = jnp.zeros((16, 128), F32)
    for k in range(2):
        total = mm(scores, hots[0][k], TN)[0:1, :] + mm(scores, hots[1][k], TN)[1:2, :]
        result = jnp.where(row == k, total, result)
    out_ref[WIDE + 64 :, :] = result.astype(BF)


def assemble_kernel(prob_in, all_ref, out_ref, prob_ref):
    for i in range(8):
        for k in range(3):
            c = WIDE * i + 128 * k
            out_ref[:, c : c + 128] = all_ref[i, 128 * k : 128 * k + 128, :]
    lane = lax.broadcasted_iota(jnp.int32, (64, 128), 1)
    for j in range(4):
        c = 8 * WIDE + 128 * j
        even = all_ref[2 * j, WIDE : WIDE + 64, :].astype(F32)
        odd = all_ref[2 * j + 1, WIDE : WIDE + 64, :].astype(F32)
        out_ref[0:64, c : c + 128] = jnp.where(lane < 64, even, pltpu.roll(odd, 64, 1)).astype(BF)
        out_ref[64:128, c : c + 128] = jnp.where(lane < 64, pltpu.roll(even, 64, 1), odd).astype(BF)
    total = all_ref[0, WIDE + 64 :, :].astype(F32)
    for i in range(1, 8):
        total = total + all_ref[i, WIDE + 64 :, :].astype(F32)
    prob_ref[...] = (total[0:2, :] / prob_in[...].astype(F32)).astype(BF)


def down_kernel(hid_ref, rows0, rows1, out_ref):
    out_ref[...] = (
        mm(hid_ref[0:ROWS, :], rows0[...], TN) + mm(hid_ref[ROWS:, :], rows1[...], TN)
    ).astype(BF)


OFFSETS = ((0, -1, 1, -2, 2, -3, 3, -4), (0, 1, -1, 2, -2, 3, -3, 4))


def hop(x, by):
    return lax.ppermute(x, "etp", [(i, (i + by) % N_Z) for i in range(N_Z)])


def ring_gather(x, way):
    shards = [x]
    far = near = x
    for step in range(4):
        far = hop(far, way)
        shards.append(far)
        if step < 3:
            near = hop(near, -way)
            shards.append(near)
    return shards


def add_rows(a, b):
    return (a.astype(F32) + b.astype(F32)).astype(BF)


def ring_scatter(packs, sums, way):
    far, near = sums
    for step in range(3):
        far = hop(add_rows(far, packs[4 - way * (step + 1)]), way)
        if step < 2:
            near = hop(add_rows(near, packs[4 + way * (step + 2)]), -way)
    return far, near


def exchange(x):
    return lax.all_to_all(x, "ep", split_axis=0, concat_axis=0, tiled=True)


def shape(*dims, dtype=BF):
    return jax.ShapeDtypeStruct(dims, dtype)


def on_device(tokens, out_grad, expert_ids, route_probs, w_gate, w_up, w_down):
    z = lax.axis_index("etp").astype(jnp.int32).reshape(1)
    ids = expert_ids.T
    probs = route_probs.T
    gate_w = w_gate[0].T
    up_w = w_up[0].T
    down_w = w_down[0]

    small = [
        pltpu.VMEM((2, TOK), jnp.int32),
        pltpu.VMEM((2, TOK), BF),
    ]
    send_ring = pl.pallas_call(
        send_ring_kernel,
        out_shape=shape(ROWS, QUARTER),
        in_specs=[SM] + [HBM] * 4,
        out_specs=VM,
        scratch_shapes=small + [pltpu.VMEM((TOK, QUARTER), BF), pltpu.SemaphoreType.DMA((3,))],
        compiler_params=params(60),
        name="send_ring",
    )(z, ids, probs, tokens, out_grad)
    got_ring = exchange(send_ring.reshape(EXPERTS, 8, QUARTER)).reshape(ROWS, QUARTER)
    send_plane = pl.pallas_call(
        send_plane_kernel,
        out_shape=shape(ROWS, 2 * D),
        in_specs=[HBM] * 4,
        out_specs=VM,
        scratch_shapes=small
        + [pltpu.VMEM((TOK, D), BF)] * 2
        + [pltpu.SemaphoreType.DMA((4,))],
        compiler_params=params(60),
        name="send_plane",
    )(ids, probs, tokens, out_grad)
    got_plane = exchange(send_plane.reshape(EXPERTS, 8, 2 * D)).reshape(ROWS, 2 * D)
    chains = ring_gather(got_ring[:128], 1) + ring_gather(got_ring[128:], -1)

    *packs, score, hidden, ring_rows = pl.pallas_call(
        functools.partial(expert_kernel, OFFSETS),
        out_shape=[shape(128, PACK)] * 16
        + [shape(2 * ROWS, 128), shape(2 * ROWS, UNITS), shape(ROWS, D)],
        in_specs=[SM] + [HBM] * 20,
        out_specs=[HBM] * 16 + [VM] * 2 + [HBM],
        scratch_shapes=[pltpu.VMEM((2, ROWS, D), BF)] * 2
        + [pltpu.VMEM((UNITS, D), BF)] * 3
        + [pltpu.VMEM((2 * ROWS, UNITS), BF)] * 2
        + [
            pltpu.VMEM((2 * ROWS, D), BF),
            pltpu.VMEM((3, ROWS, UNITS), F32),
            pltpu.VMEM((16, 128, PACK), BF),
            pltpu.SemaphoreType.DMA((2, 8)),
            pltpu.SemaphoreType.DMA((5,)),
            pltpu.SemaphoreType.DMA((17,)),
        ],
        compiler_params=params(60),
        name="expert",
    )(z, *chains, got_plane, down_w, gate_w, up_w)
    packs0, packs1 = packs[:8], packs[8:]
    sums0 = (hop(packs0[4], 1), hop(packs0[5], -1))
    sums1 = (hop(packs1[4], -1), hop(packs1[3], 1))
    back_parts = [
        packs0[0],
        *ring_scatter(packs0, sums0, 1),
        packs1[0],
        *ring_scatter(packs1, sums1, -1),
        score,
    ]

    send_back = pl.pallas_call(
        back_kernel,
        out_shape=shape(ROWS, PACK + 128),
        in_specs=[VM] * 7,
        out_specs=VM,
        compiler_params=params(),
        name="pack_back",
    )(*back_parts)
    got_back = exchange(send_back.reshape(EXPERTS, 8, PACK + 128)).reshape(ROWS, PACK + 128)
    down_grad = pl.pallas_call(
        down_kernel,
        out_shape=shape(UNITS, D),
        grid=(4,),
        in_specs=[
            pl.BlockSpec((2 * ROWS, UNITS), lambda i: (0, 0)),
            pl.BlockSpec((ROWS, QUARTER), lambda i: (0, i)),
            pl.BlockSpec((ROWS, QUARTER), lambda i: (0, 4 + i)),
        ],
        out_specs=pl.BlockSpec((UNITS, QUARTER), lambda i: (0, i)),
        compiler_params=params(),
        name="down_grad",
    )(hidden, ring_rows, got_plane)
    got_back, down_grad = lax.optimization_barrier((got_back, down_grad))
    summed = pl.pallas_call(
        token_sum_kernel,
        out_shape=shape(464, 128),
        in_specs=[VM] * 2,
        out_specs=VM,
        compiler_params=params(),
        name="token_sum",
    )(ids, got_back)
    token_grad, prob_grad = pl.pallas_call(
        assemble_kernel,
        out_shape=[shape(TOK, D), shape(2, TOK)],
        in_specs=[VM] * 2,
        out_specs=[VM] * 2,
        compiler_params=params(),
        name="assemble",
    )(probs, lax.all_gather(summed, "etp", axis=0, tiled=False))
    return (token_grad, prob_grad.T, down_grad[None])


def solution(mesh):
    return jax.shard_map(
        on_device,
        mesh=mesh,
        in_specs=(
            P("ep", None),
            P("ep", None),
            P("ep", None),
            P("ep", None),
            P("ep", None, "etp"),
            P("ep", None, "etp"),
            P("ep", "etp", None),
        ),
        out_specs=(P("ep", None), P("ep", None), P("ep", "etp", None)),
        check_vma=False,
    )
```

```python
import functools

import jax
import jax.numpy as jnp
from jax import lax
from jax.experimental import pallas as pl
from jax.experimental.pallas import tpu as pltpu
from jax.sharding import PartitionSpec as P

D = 3584
UNITS = 400
TOK = 128
EXPERTS = 32
N_Z = 8
ROWS = 256
QUARTER = D // 4
WIDE = 384
PACK = 2 * WIDE + 128
BF = jnp.bfloat16
F32 = jnp.float32

NT = (((1,), (1,)), ((), ()))
TN = (((0,), (0,)), ((), ()))
NN = (((1,), (0,)), ((), ()))


def mm(left, right, dims=NN):
    return lax.dot_general(left, right, dims, preferred_element_type=F32)


def params(mib=20):
    return pltpu.CompilerParams(vmem_limit_bytes=mib * 2**20)


VM = pl.BlockSpec(memory_space=pltpu.VMEM)
SM = pl.BlockSpec(memory_space=pltpu.SMEM)
HBM = pl.BlockSpec(memory_space=pltpu.HBM)


def slots_of(ids_ref):
    expert = lax.broadcasted_iota(jnp.int32, (EXPERTS, TOK), 0)
    first = ids_ref[0:1, :]
    second = ids_ref[1:2, :]
    hot0 = (expert == first).astype(F32)
    hot1 = (expert == second).astype(F32)
    earlier = lax.broadcasted_iota(jnp.int32, (TOK, TOK), 0) < lax.broadcasted_iota(
        jnp.int32, (TOK, TOK), 1
    )
    before = earlier.astype(BF)
    rank0 = mm(hot0.astype(BF), before)
    rank1 = mm(hot1.astype(BF), before) + jnp.sum(hot0, axis=1, keepdims=True)
    pos0 = jnp.sum(hot0 * rank0, axis=0, keepdims=True).astype(jnp.int32)
    pos1 = jnp.sum(hot1 * rank1, axis=0, keepdims=True).astype(jnp.int32)
    return first * 16 + pos0, second * 16 + pos1


def row_hot(slot, half):
    row = lax.broadcasted_iota(jnp.int32, (ROWS, TOK), 0)
    return ((row >> 3) * 16 + half * 8 + (row & 7)) == slot


def hot_of(slots, half):
    return jnp.logical_or(row_hot(slots[0], half), row_hot(slots[1], half)).astype(BF)


def prob_of(slots, prob_ref, half):
    weight = jnp.zeros((ROWS, TOK), F32)
    for k in range(2):
        weight += jnp.where(row_hot(slots[k], half), prob_ref[k : k + 1, :].astype(F32), 0.0)
    return jnp.sum(weight, axis=1, keepdims=True)


def send_ring_kernel(
    z_ref, ids_hbm, prob_hbm, tok_hbm, grad_hbm, out_ref, ids_ref, prob_ref, buf, sems
):
    z = z_ref[0]
    c_ids = pltpu.make_async_copy(ids_hbm, ids_ref, sems.at[0])
    c_prob = pltpu.make_async_copy(prob_hbm, prob_ref, sems.at[1])
    c_ids.start()
    c_prob.start()
    cols = pl.ds(pl.multiple_of(lax.rem(z, 4) * QUARTER, 128), QUARTER)
    of_tokens = pltpu.make_async_copy(tok_hbm.at[:, cols], buf, sems.at[2])
    of_grads = pltpu.make_async_copy(grad_hbm.at[:, cols], buf, sems.at[2])

    @pl.when(z < 4)
    def _():
        of_tokens.start()

    @pl.when(z >= 4)
    def _():
        of_grads.start()

    c_ids.wait()
    slots = slots_of(ids_ref)
    hot = hot_of(slots, 0)
    c_prob.wait()
    prob = jnp.where(z < 4, 1.0, prob_of(slots, prob_ref, 0))
    of_tokens.wait()
    out_ref[...] = (mm(hot, buf[...]) * prob).astype(BF)


def send_plane_kernel(
    ids_hbm, prob_hbm, tok_hbm, grad_hbm, out_ref, ids_ref, prob_ref, tok_ref, grad_ref, sems
):
    copies = [
        pltpu.make_async_copy(src, dst, sems.at[i])
        for i, (src, dst) in enumerate(
            ((ids_hbm, ids_ref), (prob_hbm, prob_ref), (tok_hbm, tok_ref), (grad_hbm, grad_ref))
        )
    ]
    for c in copies:
        c.start()
    copies[0].wait()
    slots = slots_of(ids_ref)
    hot = hot_of(slots, 1)
    copies[1].wait()
    prob = prob_of(slots, prob_ref, 1)
    copies[2].wait()
    copies[3].wait()
    for c in range(0, D, QUARTER):
        out_ref[:, c : c + QUARTER] = mm(hot, tok_ref[:, c : c + QUARTER]).astype(BF)
        out_ref[:, D + c : D + c + QUARTER] = (
            mm(hot, grad_ref[:, c : c + QUARTER]) * prob
        ).astype(BF)


def quarter(q):
    return pl.ds(q * QUARTER, QUARTER)


def expert_kernel(from_ring, z_ref, *refs):
    n = 16 if from_ring else 1
    sources, refs = refs[:n], refs[n:]
    down_hbm, gate_hbm, up_hbm = refs[:3]
    packs = refs[3:11]
    score_ref, hid_ref, rows_hbm = refs[11:14]
    rows, down_w, gate_w, up_w, part, values, row_sems, sems, out_sem = refs[14:]
    z = z_ref[0]
    row_waits = [[] for _ in range(8)]
    row_starts = []
    if from_ring:
        for chain, offsets in enumerate(OFFSETS):
            here = pl.ds(chain * 128, 128)
            for i, off in enumerate(offsets):
                owner = lax.rem(z + off + 8, 8)
                cols = pl.ds(pl.multiple_of(lax.rem(owner, 4) * QUARTER, 128), QUARTER)
                source = sources[8 * chain + i]
                row_starts.append(
                    pltpu.make_async_copy(
                        source, rows.at[owner // 4, here, cols], row_sems.at[chain, owner]
                    )
                )
                row_waits[i].append(
                    pltpu.make_async_copy(
                        source, rows.at[i // 4, here, quarter(i % 4)], row_sems.at[chain, i]
                    )
                )
    else:
        for i in range(8):
            c = pltpu.make_async_copy(
                sources[0].at[:, quarter(i)], rows.at[i // 4, :, quarter(i % 4)], row_sems.at[0, i]
            )
            row_starts.append(c)
            row_waits[i].append(c)
    weights = [
        [
            pltpu.make_async_copy(src.at[:, quarter(q)], dst.at[:, quarter(q)], sems.at[k, q])
            for q in range(4)
        ]
        for k, (src, dst) in enumerate(
            ((gate_hbm, gate_w), (up_hbm, up_w), (down_hbm, down_w))
        )
    ]
    if from_ring:
        for c in row_starts:
            c.start()
    for q in range(4):
        if not from_ring:
            row_starts[q].start()
        weights[0][q].start()
        weights[1][q].start()
    for q in range(4):
        if not from_ring:
            row_starts[4 + q].start()
        weights[2][q].start()
    for q in range(0, 4, 2):
        for p in (q, q + 1):
            for c in (*row_waits[p], weights[0][p], weights[1][p]):
                c.wait()
        cols = slice(q * QUARTER, (q + 2) * QUARTER)
        gate = mm(rows[0, :, cols], gate_w[:, cols], NT)
        up = mm(rows[0, :, cols], up_w[:, cols], NT)
        values[0] = gate if q == 0 else values[0] + gate
        values[1] = up if q == 0 else values[1] + up
    for q in range(0, 4, 2):
        for p in (q, q + 1):
            for c in (*row_waits[4 + p], weights[2][p]):
                c.wait()
        cols = slice(q * QUARTER, (q + 2) * QUARTER)
        back = mm(rows[1, :, cols], down_w[:, cols], NT)
        values[2] = back if q == 0 else values[2] + back
    if from_ring:
        rows_out = pltpu.make_async_copy(rows.at[1], rows_hbm, out_sem)
        rows_out.start()
    gate, up, back = values[0], values[1], values[2]
    sig = jax.nn.sigmoid(gate)
    hidden = (gate * sig * up).astype(BF)
    hid_ref[...] = hidden
    up_grad = (back * gate * sig).astype(BF)
    gate_grad = (back * up * sig * (1.0 + gate * (1.0 - sig))).astype(BF)
    score = jnp.sum(back * hidden.astype(F32), axis=1, keepdims=True)
    score_ref[...] = jnp.broadcast_to(score, (ROWS, 128)).astype(BF)
    for c in range(0, D, QUARTER):
        part[:, c : c + QUARTER] = (
            mm(gate_grad, gate_w[:, c : c + QUARTER]) + mm(up_grad, up_w[:, c : c + QUARTER])
        ).astype(BF)
    lane = lax.broadcasted_iota(jnp.int32, (128, 128), 1)
    for r in range(8):
        shard = lax.rem(z + r, 8)
        cols = pl.ds(pl.multiple_of(shard * WIDE, 128), WIDE)
        tile = pl.ds(pl.multiple_of((24 + shard // 2) * 128, 128), 128)
        odd = lax.rem(shard, 2) == 1
        packs[r][:, :WIDE] = part[0:128, cols]
        packs[r][:, WIDE : 2 * WIDE] = part[128:256, cols]
        top = part[0:128, tile].astype(F32)
        bottom = part[128:256, tile].astype(F32)
        top = jnp.where(odd, pltpu.roll(top, 64, 1), top)
        bottom = jnp.where(odd, bottom, pltpu.roll(bottom, 64, 1))
        packs[r][:, 2 * WIDE :] = jnp.where(lane < 64, top, bottom).astype(BF)
    if from_ring:
        rows_out.wait()


def back_kernel(*refs):
    out_ref = refs[8]
    lane = lax.broadcasted_iota(jnp.int32, (128, 128), 1)
    tiles = []
    for half in range(2):
        own, left, right = refs[3 * half : 3 * half + 3]
        total = (
            own[...].astype(F32) + left[...].astype(F32) + right[...].astype(F32)
        )
        base = half * WIDE
        out_ref[0:128, base : base + WIDE] = total[:, :WIDE].astype(BF)
        out_ref[128:256, base : base + WIDE] = total[:, WIDE : 2 * WIDE].astype(BF)
        tile = total[:, 2 * WIDE :]
        tiles.append((tile, pltpu.roll(tile, 64, 1)))
    (t0, r0), (t1, r1) = tiles
    out_ref[0:128, 2 * WIDE : PACK] = jnp.where(lane < 64, t0, r1).astype(BF)
    out_ref[128:256, 2 * WIDE : PACK] = jnp.where(lane < 64, r0, t1).astype(BF)
    score0, score1 = refs[6][...], refs[7][...]
    wide = lax.broadcasted_iota(jnp.int32, (ROWS, 128), 1)
    out_ref[:, PACK:] = jnp.where(
        wide == 0, score0.astype(F32), jnp.where(wide == 1, score1.astype(F32), 0.0)
    ).astype(BF)


def token_sum_kernel(ids_ref, got_ref, out_ref):
    slot0, slot1 = slots_of(ids_ref)
    hots = [
        [row_hot(slot, half).astype(BF) for slot in (slot0, slot1)] for half in range(2)
    ]
    both = [h[0] + h[1] for h in hots]
    wide = mm(both[0], got_ref[:, :WIDE], TN) + mm(both[1], got_ref[:, WIDE : 2 * WIDE], TN)
    for k in range(3):
        out_ref[128 * k : 128 * k + 128, :] = wide[:, 128 * k : 128 * k + 128].astype(BF)
    tile = got_ref[:, 2 * WIDE : PACK]
    half_tile = mm(both[0], tile, TN) + pltpu.roll(mm(both[1], tile, TN), 64, 1)
    lane = lax.broadcasted_iota(jnp.int32, (64, 128), 1)
    out_ref[WIDE : WIDE + 64, :] = jnp.where(
        lane < 64, half_tile[:64], pltpu.roll(half_tile[64:], 64, 1)
    ).astype(BF)
    scores = got_ref[:, PACK:]
    row = lax.broadcasted_iota(jnp.int32, (16, 128), 0)
    result = jnp.zeros((16, 128), F32)
    for k in range(2):
        total = mm(scores, hots[0][k], TN)[0:1, :] + mm(scores, hots[1][k], TN)[1:2, :]
        result = jnp.where(row == k, total, result)
    out_ref[WIDE + 64 :, :] = result.astype(BF)


def assemble_kernel(prob_in, all_ref, out_ref, prob_ref):
    for i in range(8):
        for k in range(3):
            c = WIDE * i + 128 * k
            out_ref[:, c : c + 128] = all_ref[i, 128 * k : 128 * k + 128, :]
    lane = lax.broadcasted_iota(jnp.int32, (64, 128), 1)
    for j in range(4):
        c = 8 * WIDE + 128 * j
        even = all_ref[2 * j, WIDE : WIDE + 64, :].astype(F32)
        odd = all_ref[2 * j + 1, WIDE : WIDE + 64, :].astype(F32)
        out_ref[0:64, c : c + 128] = jnp.where(lane < 64, even, pltpu.roll(odd, 64, 1)).astype(BF)
        out_ref[64:128, c : c + 128] = jnp.where(lane < 64, pltpu.roll(even, 64, 1), odd).astype(BF)
    total = all_ref[0, WIDE + 64 :, :].astype(F32)
    for i in range(1, 8):
        total = total + all_ref[i, WIDE + 64 :, :].astype(F32)
    prob_ref[...] = (total[0:2, :] / prob_in[...].astype(F32)).astype(BF)


def down_kernel(hid0, hid1, rows0, rows1, out_ref):
    out_ref[...] = (
        mm(hid0[...], rows0[...], TN) + mm(hid1[...], rows1[...], TN)
    ).astype(BF)


OFFSETS = ((0, -1, 1, -2, 2, -3, 3, -4), (0, 1, -1, 2, -2, 3, -3, 4))


def hop(x, by):
    return lax.ppermute(x, "etp", [(i, (i + by) % N_Z) for i in range(N_Z)])


def ring_gather(x, way):
    shards = [x]
    far = near = x
    for step in range(4):
        far = hop(far, way)
        shards.append(far)
        if step < 3:
            near = hop(near, -way)
            shards.append(near)
    return shards


def add_rows(a, b):
    return (a.astype(F32) + b.astype(F32)).astype(BF)


def ring_scatter(packs, sums, way):
    far, near = sums
    for step in range(3):
        far = hop(add_rows(far, packs[4 - way * (step + 1)]), way)
        if step < 2:
            near = hop(add_rows(near, packs[4 + way * (step + 2)]), -way)
    return far, near


def exchange(x):
    return lax.all_to_all(x, "ep", split_axis=0, concat_axis=0, tiled=True)


def shape(*dims, dtype=BF):
    return jax.ShapeDtypeStruct(dims, dtype)


def on_device(tokens, out_grad, expert_ids, route_probs, w_gate, w_up, w_down):
    z = lax.axis_index("etp").astype(jnp.int32).reshape(1)
    ids = expert_ids.T
    probs = route_probs.T
    gate_w = w_gate[0].T
    up_w = w_up[0].T
    down_w = w_down[0]

    small = [
        pltpu.VMEM((2, TOK), jnp.int32),
        pltpu.VMEM((2, TOK), BF),
    ]
    send_ring = pl.pallas_call(
        send_ring_kernel,
        out_shape=shape(ROWS, QUARTER),
        in_specs=[SM] + [HBM] * 4,
        out_specs=VM,
        scratch_shapes=small + [pltpu.VMEM((TOK, QUARTER), BF), pltpu.SemaphoreType.DMA((3,))],
        compiler_params=params(60),
        name="send_ring",
    )(z, ids, probs, tokens, out_grad)
    got_ring = exchange(send_ring.reshape(EXPERTS, 8, QUARTER)).reshape(ROWS, QUARTER)
    send_plane = pl.pallas_call(
        send_plane_kernel,
        out_shape=shape(ROWS, 2 * D),
        in_specs=[HBM] * 4,
        out_specs=VM,
        scratch_shapes=small
        + [pltpu.VMEM((TOK, D), BF)] * 2
        + [pltpu.SemaphoreType.DMA((4,))],
        compiler_params=params(60),
        name="send_plane",
    )(ids, probs, tokens, out_grad)
    got_plane = exchange(send_plane.reshape(EXPERTS, 8, 2 * D)).reshape(ROWS, 2 * D)
    chains = ring_gather(got_ring[:128], 1) + ring_gather(got_ring[128:], -1)

    def expert(from_ring, sources):
        return pl.pallas_call(
            functools.partial(expert_kernel, from_ring),
            out_shape=[shape(128, PACK)] * 8
            + [shape(ROWS, 128), shape(ROWS, UNITS), shape(ROWS, D if from_ring else 128)],
            in_specs=[SM] + [HBM] * (len(sources) + 3),
            out_specs=[VM] * 10 + [HBM],
            scratch_shapes=[pltpu.VMEM((2, ROWS, D), BF)]
            + [pltpu.VMEM((UNITS, D), BF)] * 3
            + [
                pltpu.VMEM((ROWS, D), BF),
                pltpu.VMEM((3, ROWS, UNITS), F32),
                pltpu.SemaphoreType.DMA((2, 8)),
                pltpu.SemaphoreType.DMA((3, 4)),
                pltpu.SemaphoreType.DMA(()),
            ],
            compiler_params=params(60),
            name="ring_expert" if from_ring else "plane_expert",
        )(z, *sources, down_w, gate_w, up_w)

    *packs0, score0, hidden0, ring_rows = expert(True, chains)
    sums0 = (hop(packs0[4], 1), hop(packs0[5], -1))
    *packs1, score1, hidden1, _ = expert(False, [got_plane])
    sums0, packs1 = lax.optimization_barrier((sums0, packs1))
    sums1 = (hop(packs1[4], -1), hop(packs1[3], 1))
    back_parts = [
        packs0[0],
        *ring_scatter(packs0, sums0, 1),
        packs1[0],
        *ring_scatter(packs1, sums1, -1),
        score0,
        score1,
    ]

    send_back = pl.pallas_call(
        back_kernel,
        out_shape=shape(ROWS, PACK + 128),
        in_specs=[VM] * 8,
        out_specs=VM,
        compiler_params=params(),
        name="pack_back",
    )(*back_parts)
    got_back = exchange(send_back.reshape(EXPERTS, 8, PACK + 128)).reshape(ROWS, PACK + 128)
    down_grad = pl.pallas_call(
        down_kernel,
        out_shape=shape(UNITS, D),
        grid=(4,),
        in_specs=[
            pl.BlockSpec((ROWS, UNITS), lambda i: (0, 0)),
            pl.BlockSpec((ROWS, UNITS), lambda i: (0, 0)),
            pl.BlockSpec((ROWS, QUARTER), lambda i: (0, i)),
            pl.BlockSpec((ROWS, QUARTER), lambda i: (0, 4 + i)),
        ],
        out_specs=pl.BlockSpec((UNITS, QUARTER), lambda i: (0, i)),
        compiler_params=params(),
        name="down_grad",
    )(hidden0, hidden1, ring_rows, got_plane)
    got_back, down_grad = lax.optimization_barrier((got_back, down_grad))
    summed = pl.pallas_call(
        token_sum_kernel,
        out_shape=shape(464, 128),
        in_specs=[VM] * 2,
        out_specs=VM,
        compiler_params=params(),
        name="token_sum",
    )(ids, got_back)
    token_grad, prob_grad = pl.pallas_call(
        assemble_kernel,
        out_shape=[shape(TOK, D), shape(2, TOK)],
        in_specs=[VM] * 2,
        out_specs=[VM] * 2,
        compiler_params=params(),
        name="assemble",
    )(probs, lax.all_gather(summed, "etp", axis=0, tiled=False))
    return (token_grad, prob_grad.T, down_grad[None])


def solution(mesh):
    return jax.shard_map(
        on_device,
        mesh=mesh,
        in_specs=(
            P("ep", None),
            P("ep", None),
            P("ep", None),
            P("ep", None),
            P("ep", None, "etp"),
            P("ep", None, "etp"),
            P("ep", "etp", None),
        ),
        out_specs=(P("ep", None), P("ep", None), P("ep", "etp", None)),
        check_vma=False,
    )
```
